256 devices in a mesh: gx: 64 (over z_hi, x, y), gy: 4 (over z_lo, core).
Axes of the slice: x: 4, y: 4, z: 8 (z_hi: 4, z_lo: 2; z = z_hi * 2 + z_lo), core: 2. Of those that a mesh axis runs over, the one named last changes fastest.
Arguments:
- density: float32 [4096, 32768], P('gx', 'gy'), may hold values from -6 to 6
- kz_square: float32 [8], replicated, may hold values from 0.25 to 4
Outputs:
- potential: float32 [2, 2048, 8, 4096], P(None, ('gx', 'gy'))
The draws below stay inside these ranges and needn't reach their ends.
All inputs are finite; a program needn't handle non-finite values.
Results may differ from the reference program's by a relative error of at most 0.000071.
Values sent between devices are 32-bit elements; how exact they have to be, the bound alone decides.
No kernel may reach another device: no remote copies, remote signals or barrier semaphores. Data moves between devices by JAX's collectives and lax.ppermute only.
A program may use at most 64 MiB of HBM per device.

```python
import math
import jax
import jax.numpy as jnp
from jax import lax

NX = 4096
NY = 4096
PLANES = 8
KX = 2048


def levels(key, extent, shards, low, largest):
    def one(position, shards_of):
        steps = jax.random.uniform(jax.random.fold_in(jax.random.fold_in(key, 6), position), (shards_of,), jnp.float32, low / len(shards), largest / len(shards))
        return jnp.repeat(jnp.exp(steps), extent[position] // shards_of).reshape((-1,) + (1,) * (len(extent) - position - 1))

    loudness = one(*shards[0])
    for cut in shards[1:]:
        loudness = loudness * one(*cut)
    return loudness


def bell_draw(stream_key, shape, spread, limit, cuts=(), held_as=jnp.bfloat16):
    drawn = jax.random.normal(stream_key, shape, jnp.float32) * spread
    if len(cuts) > 0:
        drawn = levels(stream_key, shape, cuts, -0.22, 0.18) * drawn
    return jnp.clip(drawn, min=-limit, max=limit).astype(held_as)


def setup_inputs(seed: int = 0) -> dict:
    keys = jax.random.split(jax.random.key(seed), 3)
    return {
        "density": bell_draw(keys[0], (NX, NY * PLANES), 1.0, 6.0, ((0, 64), (1, 4)), jnp.float32),
        "kz_square": jnp.clip(jnp.exp(jax.random.uniform(keys[1], (PLANES,), jnp.float32, math.log(0.25), math.log(4.0))), 0.25, 4.0),
    }


def reference(density, kz_square):
    grid_field = density.reshape(NX, NY, PLANES)
    wave_x = jnp.arange(KX).astype(jnp.float32)
    wave_y = jnp.arange(NY).astype(jnp.float32)
    symbol_x = 4.0 * jnp.sin(wave_x * (math.pi / NX)) ** 2
    symbol_y = 4.0 * jnp.sin(wave_y * (math.pi / NY)) ** 2
    norm_scale = 1.0 / math.sqrt(NX * NY)

    def one_plane(plane_index):
        plane_data = lax.dynamic_index_in_dim(grid_field, plane_index, axis=2, keepdims=False)
        spectrum = jnp.fft.rfft(plane_data, axis=0)[:KX]
        transformed = jnp.fft.fft(spectrum, axis=1)
        kz_value = lax.dynamic_index_in_dim(kz_square, plane_index, 0, False)
        denominator = symbol_x[:, None] + symbol_y[None, :] + kz_value
        result = -(transformed * norm_scale) / denominator
        return jnp.stack([jnp.real(result), jnp.imag(result)])
    planes_out = lax.map(one_plane, jnp.arange(PLANES, dtype=jnp.int32))
    return jnp.transpose(planes_out, (1, 2, 0, 3))
```

```python
import functools
import math

import jax
import jax.numpy as jnp
import ml_dtypes
import numpy as np
from jax import lax
from jax.experimental import pallas as pl
from jax.experimental.pallas import tpu as pltpu
from jax.sharding import Mesh
from jax.sharding import PartitionSpec as P

LENGTH = 4096
KEPT = 2048
ROOT = 64
LANES = 128
HALF = 64
PLANES = 8
AXES = ("zh", "x", "y", "zl", "core")


def split_table(table, axis, order):
    high = table.astype(ml_dtypes.bfloat16)
    low = (table - high.astype(np.float64)).astype(ml_dtypes.bfloat16)
    parts = {"h": high, "l": low}
    return np.concatenate([parts[name] for name in order], axis=axis)


def split_data(values, axis, order):
    high = values.astype(jnp.bfloat16)
    low = (values - high.astype(jnp.float32)).astype(jnp.bfloat16)
    parts = {"h": high, "l": low}
    return jnp.concatenate([parts[name] for name in order], axis=axis)


@functools.cache
def x_tables():
    a = np.arange(ROOT)
    first = 2.0 * np.pi * np.outer(np.arange(ROOT // 2 + 1), a) / ROOT
    outer = np.concatenate([np.cos(first), -np.sin(first[1 : ROOT // 2])], axis=0)
    sections = []
    k2 = np.arange(KEPT // ROOT)
    for k1 in range(ROOT // 2 + 1):
        angle = 2.0 * np.pi * np.outer(k1 + ROOT * k2, a) / LENGTH
        rows = [np.concatenate([np.cos(angle), -np.sin(angle)], axis=1)]
        mirror = 2.0 * np.pi * np.outer((ROOT - k1) % ROOT + ROOT * k2, a) / LENGTH
        rows.append(np.concatenate([np.cos(mirror), np.sin(mirror)], axis=1))
        sections.append(np.concatenate(rows, axis=0))
    return split_table(outer, 1, "hhl"), split_table(np.stack(sections), 2, "hhl")


@functools.cache
def y_tables():
    source = np.arange(256)
    place = (source % 4) * 64 + source // 4
    angle = 2.0 * np.pi * np.outer(place, np.arange(256)) / 256
    table = np.concatenate([np.cos(angle), -np.sin(angle)], axis=1)
    turn = 2.0 * np.pi * np.outer(np.arange(16), np.arange(256)) / LENGTH
    wave = np.arange(LENGTH).reshape(16, 256)
    symbol = 4.0 * np.sin(np.pi * wave / LENGTH) ** 2
    return (
        split_table(table, 0, "hhl"),
        np.cos(turn).astype(np.float32),
        (-np.sin(turn)).astype(np.float32),
        symbol.astype(np.float32),
    )


def x_kernel(outer_ref, section_ref, lines_ref, out_ref, mixed_ref):
    outer = outer_ref[...]
    for b in range(0, ROOT, 2):
        pair = jnp.concatenate(
            [lines_ref[pl.ds(b + i, ROOT, stride=ROOT), :] for i in range(2)], axis=1
        )
        mixed = jnp.dot(outer, split_data(pair, 0, "hlh"), preferred_element_type=jnp.float32)
        for i in range(2):
            mixed_ref[pl.ds(b + i, ROOT, stride=ROOT), :] = mixed[:, i * LANES : (i + 1) * LANES]
    left = lax.broadcasted_iota(jnp.int32, (ROOT, LANES), 1) < HALF
    keep = lax.broadcasted_iota(jnp.int32, (KEPT // ROOT, 2 * LANES), 1) % LANES < HALF
    for k1 in range(ROOT // 2 + 1):
        real = mixed_ref[k1 * ROOT : (k1 + 1) * ROOT, :]
        real_turned = pltpu.roll(real, HALF, 1)
        if 0 < k1 < ROOT // 2:
            imag = mixed_ref[(ROOT // 2 + k1) * ROOT : (ROOT // 2 + k1 + 1) * ROOT, :]
            imag_turned = pltpu.roll(imag, HALF, 1)
        else:
            imag = jnp.zeros_like(real)
            imag_turned = imag
        upper = jnp.concatenate(
            [jnp.where(left, real, imag_turned), jnp.where(left, real_turned, imag)], axis=1
        )
        lower = jnp.concatenate(
            [jnp.where(left, -imag, real_turned), jnp.where(left, -imag_turned, real)], axis=1
        )
        data = split_data(jnp.concatenate([upper, lower], axis=0), 0, "hlh")
        result = jnp.dot(section_ref[k1], data, preferred_element_type=jnp.float32)
        count = KEPT // ROOT
        for h in range(2):
            start = (k1 // 8) * 16 + h * 8 + k1 % 8
            out_ref[pl.ds(start, count, stride=LANES), :] = result[:count, h * LANES : (h + 1) * LANES]
        if 0 < k1 < ROOT // 2:
            other = ROOT - k1
            mirrored = jnp.where(keep, result[count:], -result[count:])
            for h in range(2):
                start = (other // 8) * 16 + h * 8 + other % 8
                out_ref[pl.ds(start, count, stride=LANES), :] = mirrored[:, h * LANES : (h + 1) * LANES]


def x_transform(lines):
    outer, sections = x_tables()
    return pl.pallas_call(
        x_kernel,
        out_shape=jax.ShapeDtypeStruct((LENGTH, LANES), jnp.float32),
        scratch_shapes=[pltpu.VMEM((LENGTH, LANES), jnp.float32)],
        compiler_params=pltpu.CompilerParams(vmem_limit_bytes=40 << 20),
        name="x_transform",
    )(jnp.asarray(outer), jnp.asarray(sections), lines)


def add(p, q):
    return (p[0] + q[0], p[1] + q[1])


def sub(p, q):
    return (p[0] - q[0], p[1] - q[1])


def turn_back(p):
    return (p[1], -p[0])


def times(p, angle):
    cosine, sine_part = math.cos(angle), math.sin(angle)
    return (p[0] * cosine - p[1] * sine_part, p[1] * cosine + p[0] * sine_part)


def four(p, q, r, s):
    even, odd = add(p, r), add(q, s)
    even_minus, odd_minus = sub(p, r), turn_back(sub(q, s))
    return add(even, odd), add(even_minus, odd_minus), sub(even, odd), sub(even_minus, odd_minus)


def sixteen(values):
    columns = []
    for n in range(4):
        column = four(*[values[4 * m + n] for m in range(4)])
        columns.append([times(v, -2.0 * math.pi * n * k / 16) if n * k else v for k, v in enumerate(column)])
    out = [None] * 16
    for k in range(4):
        for l, v in enumerate(four(*[columns[n][k] for n in range(4)])):
            out[k + 4 * l] = v
    return out


def y_kernel(symbol_x_ref, table_ref, cosine_ref, sine_ref, symbol_ref, kz_ref, lines_ref, out_ref):
    table = table_ref[...]
    scale = -1.0 / math.sqrt(LENGTH * LENGTH)
    kz = kz_ref[...]
    for j in range(8):
        rows = []
        for h in range(2):
            values = lines_ref[pl.ds(h * 8 + j, 256, stride=16), :]
            rows.append(split_data(values.T, 1, "hlh"))
        product = jnp.dot(jnp.concatenate(rows, axis=0), table, preferred_element_type=jnp.float32)
        values = []
        for h in range(2):
            for m in range(8):
                first = product[h * LANES + m * 8 : h * LANES + m * 8 + 8]
                second = product[h * LANES + HALF + m * 8 : h * LANES + HALF + m * 8 + 8]
                real = first[:, :256] - second[:, 256:]
                imag = first[:, 256:] + second[:, :256]
                n = h * 8 + m
                if n:
                    cosine, sine_part = cosine_ref[n : n + 1, :], sine_ref[n : n + 1, :]
                    real, imag = real * cosine - imag * sine_part, imag * cosine + real * sine_part
                values.append((real, imag))
        shift = kz + symbol_x_ref[j]
        for k, (real, imag) in enumerate(sixteen(values)):
            factor = scale / (shift + symbol_ref[k : k + 1, :])
            out_ref[0, j, :, k * 256 : (k + 1) * 256] = real * factor
            out_ref[1, j, :, k * 256 : (k + 1) * 256] = imag * factor


def y_transform(lines, symbol_x, kz_square):
    table, cosine, sine_part, symbol = y_tables()
    vmem = pl.BlockSpec(memory_space=pltpu.VMEM)
    return pl.pallas_call(
        y_kernel,
        out_shape=jax.ShapeDtypeStruct((2, 8, PLANES, LENGTH), jnp.float32),
        in_specs=[pl.BlockSpec(memory_space=pltpu.SMEM)] + [vmem] * 6,
        compiler_params=pltpu.CompilerParams(vmem_limit_bytes=40 << 20),
        name="y_transform",
    )(
        symbol_x,
        jnp.asarray(table),
        jnp.asarray(cosine),
        jnp.asarray(sine_part),
        jnp.asarray(symbol),
        jnp.broadcast_to(kz_square[:, None], (PLANES, 256)),
        lines,
    )


def body(density, kz_square):
    gx = AXES[:3]
    blocks = jnp.transpose(density.reshape(64, 64, LANES), (1, 0, 2))
    lines = lax.all_to_all(blocks, gx, 0, 0, tiled=True)
    spectrum = x_transform(lines.reshape(LENGTH, LANES))
    lines = lax.all_to_all(spectrum.reshape(256, 16, LANES), AXES, 0, 0, tiled=True)
    wave_x = (lax.axis_index(AXES) * 8 + jnp.arange(8, dtype=jnp.int32)).astype(jnp.float32)
    symbol_x = 4.0 * jnp.sin(wave_x * (math.pi / LENGTH)) ** 2
    return y_transform(lines.reshape(LENGTH, LANES), symbol_x, kz_square)


def solution(mesh):
    fine = Mesh(mesh.devices.reshape(4, 4, 4, 2, 2), AXES)
    in_specs = (P(AXES[:3], AXES[3:]), P())
    out_specs = P(None, AXES, None, None)
    return jax.shard_map(body, mesh=fine, in_specs=in_specs, out_specs=out_specs, check_vma=False)
```

```python
import functools
import math

import jax
import jax.numpy as jnp
import ml_dtypes
import numpy as np
from jax import lax
from jax.experimental import pallas as pl
from jax.experimental.pallas import tpu as pltpu
from jax.sharding import Mesh
from jax.sharding import PartitionSpec as P

LENGTH = 4096
KEPT = 2048
ROOT = 64
LANES = 128
HALF = 64
PLANES = 8
ROWS = 32
SLOT = 256
AXES = ("zh", "x", "y", "zl", "core")


def split_table(table, axis, order):
    high = table.astype(ml_dtypes.bfloat16)
    low = (table - high.astype(np.float64)).astype(ml_dtypes.bfloat16)
    parts = {"h": high, "l": low}
    return np.concatenate([parts[name] for name in order], axis=axis)


def split_data(values, axis, order):
    high = values.astype(jnp.bfloat16)
    low = (values - high.astype(jnp.float32)).astype(jnp.bfloat16)
    parts = {"h": high, "l": low}
    return jnp.concatenate([parts[name] for name in order], axis=axis)


@functools.cache
def x_tables():
    a = np.arange(ROOT)
    first = 2.0 * np.pi * np.outer(np.arange(ROOT // 2 + 1), a) / ROOT
    outer = np.concatenate([np.cos(first), -np.sin(first[1 : ROOT // 2])], axis=0)
    sections = []
    k2 = np.arange(KEPT // ROOT)
    for k1 in range(ROOT // 2 + 1):
        angle = 2.0 * np.pi * np.outer(k1 + ROOT * k2, a) / LENGTH
        rows = [np.concatenate([np.cos(angle), -np.sin(angle)], axis=1)]
        mirror = 2.0 * np.pi * np.outer((ROOT - k1) % ROOT + ROOT * k2, a) / LENGTH
        rows.append(np.concatenate([np.cos(mirror), np.sin(mirror)], axis=1))
        sections.append(np.concatenate(rows, axis=0))
    return split_table(outer, 1, "hhl"), split_table(np.stack(sections), 2, "hhl")


@functools.cache
def y_tables():
    source = np.arange(256)
    zh, zl, xy, core = source // 64, source // 32 % 2, source // 2 % 16, source % 2
    place = (zl * 2 + core) * 64 + zh * 16 + xy
    angle = 2.0 * np.pi * np.outer(place, np.arange(256)) / 256
    table = np.concatenate([np.cos(angle), -np.sin(angle)], axis=1)
    turn = 2.0 * np.pi * np.outer(np.arange(16), np.arange(256)) / LENGTH
    wave = np.arange(LENGTH).reshape(16, 256)
    symbol = 4.0 * np.sin(np.pi * wave / LENGTH) ** 2
    return (
        split_table(table, 0, "hhl"),
        np.cos(turn).astype(np.float32),
        (-np.sin(turn)).astype(np.float32),
        symbol.astype(np.float32),
    )


def left_lanes(rows):
    return lax.broadcasted_iota(jnp.int32, (rows, LANES), 1) < HALF


def pack_kernel(place_ref, density_ref, *out_refs):
    zh = place_ref[0]
    left = left_lanes(ROWS)
    for dz in range(4):
        base = ((zh + dz) & 3) * (16 * LANES)
        for xy in range(16):
            start = pl.multiple_of(base + xy * LANES, LANES)
            upper = density_ref[:ROWS, pl.ds(start, LANES)]
            lower = density_ref[ROWS:, pl.ds(start, LANES)]
            out_refs[dz][xy] = jnp.where(left, upper, pltpu.roll(lower, HALF, 1))
            out_refs[4][xy, dz] = jnp.where(left, pltpu.roll(upper, HALF, 1), lower)


def join_kernel(*refs):
    for slot, ref in enumerate(refs[:-1]):
        refs[-1][:, slot] = ref[...]


def split_kernel(in_ref, *out_refs):
    for slot, ref in enumerate(out_refs):
        ref[...] = in_ref[:, slot]


def call(kernel, name, out_shape, scalars, *arrays, scratch=()):
    vmem = pl.BlockSpec(memory_space=pltpu.VMEM)
    smem = pl.BlockSpec(memory_space=pltpu.SMEM)
    return pl.pallas_call(
        kernel,
        out_shape=out_shape,
        in_specs=[smem] * len(scalars) + [vmem] * len(arrays),
        scratch_shapes=list(scratch),
        compiler_params=pltpu.CompilerParams(vmem_limit_bytes=40 << 20),
        name=name,
    )(*scalars, *arrays)


def floats(*shape):
    return jax.ShapeDtypeStruct(shape, jnp.float32)


def pack(density, place):
    out_shape = [floats(16, ROWS, LANES)] * 4 + [floats(16, 4, ROWS, LANES)]
    return call(pack_kernel, "pack", out_shape, [place], density)


def join(parts):
    n, rows, lanes = parts[0].shape
    return call(join_kernel, "join", floats(n, len(parts), rows, lanes), [], *parts)


def split(whole):
    n, count, rows, lanes = whole.shape
    return call(split_kernel, "split", [floats(n, rows, lanes)] * count, [], whole)


def x_steps(outer, section_ref, load_row, mixed_ref, store):
    for r in range(0, ROWS, 2):
        pair = jnp.concatenate([load_row(r), load_row(r + 1)], axis=1)
        mixed = jnp.dot(outer, split_data(pair, 0, "hlh"), preferred_element_type=jnp.float32)
        for i in range(2):
            mixed_ref[pl.ds(r + i, ROOT, stride=ROWS), :] = mixed[:, i * LANES : (i + 1) * LANES]
    left = left_lanes(ROWS)
    for k1 in range(ROOT // 2 + 1):
        real = mixed_ref[k1 * ROWS : (k1 + 1) * ROWS, :]
        real_turned = pltpu.roll(real, HALF, 1)
        if 0 < k1 < ROOT // 2:
            imag = mixed_ref[(ROOT // 2 + k1) * ROWS : (ROOT // 2 + k1 + 1) * ROWS, :]
            imag_turned = pltpu.roll(imag, HALF, 1)
        else:
            imag = jnp.zeros_like(real)
            imag_turned = imag
        data = jnp.concatenate(
            [
                jnp.where(left, real, imag_turned),
                jnp.where(left, real_turned, imag),
                jnp.where(left, -imag, real_turned),
                jnp.where(left, -imag_turned, real),
            ],
            axis=0,
        )
        result = jnp.dot(section_ref[k1], split_data(data, 0, "hlh"), preferred_element_type=jnp.float32)
        count = KEPT // ROOT
        store(k1, result[:count])
        if 0 < k1 < ROOT // 2:
            store(ROOT - k1, jnp.where(left, result[count:], -result[count:]))


def x_first_kernel(place_ref, outer_ref, section_ref, lines_ref, *refs):
    out_refs, mixed_ref, slots_ref = refs[:8], refs[8], refs[9]
    zh, z = place_ref[0], place_ref[1]

    def load_row(r):
        parts = []
        for source in range(4):
            start = ((zh - source) & 3) * ROWS + r
            parts.append(lines_ref[pl.ds(start, 16, stride=4 * ROWS), :])
        return jnp.concatenate(parts, axis=0)

    def store(k1, values):
        for zh_out in range(4):
            slot = (2 * zh_out + (k1 >> 4 & 1) - z) & 7
            start = slot * SLOT + ((k1 >> 5) * 2 + (k1 >> 3 & 1)) * 8 + k1 % 8
            slots_ref[pl.ds(start, 8, stride=32), :] = values[zh_out * 8 : zh_out * 8 + 8]

    x_steps(outer_ref[...], section_ref, load_row, mixed_ref, store)
    for slot in range(8):
        out_refs[slot][...] = slots_ref[slot * SLOT : (slot + 1) * SLOT, :].reshape(32, 8, LANES)


def x_second_kernel(place_ref, outer_ref, section_ref, *refs):
    in_refs, out_ref, mixed_ref, lines_ref = refs[:4], refs[4], refs[5], refs[6]
    zh, z = place_ref[0], place_ref[1]
    for dz in range(4):
        start = pl.multiple_of(((zh - dz) & 3) * (16 * ROWS), 16 * ROWS)
        lines_ref[pl.ds(start, 16 * ROWS), :] = in_refs[dz][...].reshape(16 * ROWS, LANES)

    def load_row(r):
        return lines_ref[pl.ds(r, ROOT, stride=ROWS), :]

    def store(k1, values):
        for zh_out in range(4):
            slot = (2 * zh_out + (k1 >> 4 & 1) - z) & 7
            start = (((k1 >> 5) * 2 + (k1 >> 3 & 1)) * 8 + slot) * 8 + k1 % 8
            out_ref[pl.ds(start, 8, stride=SLOT), :] = values[zh_out * 8 : zh_out * 8 + 8]

    x_steps(outer_ref[...], section_ref, load_row, mixed_ref, store)


def x_transform_first(lines, place):
    outer, sections = x_tables()
    lines = lines.reshape(ROOT * ROWS, LANES)
    scratch = [pltpu.VMEM((ROOT * ROWS, LANES), jnp.float32)] * 2
    tables = [jnp.asarray(outer), jnp.asarray(sections)]
    return call(x_first_kernel, "x_first", [floats(32, 8, LANES)] * 8, [place], *tables, lines, scratch=scratch)


def x_transform_second(parts, place):
    outer, sections = x_tables()
    scratch = [pltpu.VMEM((ROOT * ROWS, LANES), jnp.float32)] * 2
    tables = [jnp.asarray(outer), jnp.asarray(sections)]
    out = call(x_second_kernel, "x_second", floats(8 * SLOT, LANES), [place], *tables, *parts, scratch=scratch)
    return out.reshape(32, 8, 8, LANES)


def add(p, q):
    return (p[0] + q[0], p[1] + q[1])


def sub(p, q):
    return (p[0] - q[0], p[1] - q[1])


def turn_back(p):
    return (p[1], -p[0])


def times(p, angle):
    cosine, sine_part = math.cos(angle), math.sin(angle)
    return (p[0] * cosine - p[1] * sine_part, p[1] * cosine + p[0] * sine_part)


def four(p, q, r, s):
    even, odd = add(p, r), add(q, s)
    even_minus, odd_minus = sub(p, r), turn_back(sub(q, s))
    return add(even, odd), add(even_minus, odd_minus), sub(even, odd), sub(even_minus, odd_minus)


def sixteen(values):
    columns = []
    for n in range(4):
        column = four(*[values[4 * m + n] for m in range(4)])
        columns.append([times(v, -2.0 * math.pi * n * k / 16) if n * k else v for k, v in enumerate(column)])
    out = [None] * 16
    for k in range(4):
        for l, v in enumerate(four(*[columns[n][k] for n in range(4)])):
            out[k + 4 * l] = v
    return out


def y_kernel(place_ref, symbol_x_ref, table_ref, cosine_ref, sine_ref, symbol_ref, kz_ref, first_ref, *refs):
    second_refs, out_ref, lines_ref = refs[:8], refs[8], refs[9]
    z = place_ref[1]
    for dz in range(8):
        start = pl.multiple_of(((z - dz) & 7) * SLOT, SLOT)
        lines_ref[pl.ds(start, SLOT), :] = second_refs[dz][...].reshape(SLOT, LANES)
    table = table_ref[...]
    scale = -1.0 / math.sqrt(LENGTH * LENGTH)
    kz = kz_ref[...]
    for j in range(8):
        parts = [first_ref[pl.ds(((z - source) & 7) * 8 + j, 32, stride=64), :] for source in range(8)]
        halves = [jnp.concatenate(parts, axis=0), lines_ref[pl.ds(j, 256, stride=8), :]]
        rows = jnp.concatenate([split_data(half.T, 1, "hlh") for half in halves], axis=0)
        product = jnp.dot(rows, table, preferred_element_type=jnp.float32)
        values = []
        for h in range(2):
            for m in range(8):
                first = product[h * LANES + m * 8 : h * LANES + m * 8 + 8]
                second = product[h * LANES + HALF + m * 8 : h * LANES + HALF + m * 8 + 8]
                real = first[:, :256] - second[:, 256:]
                imag = first[:, 256:] + second[:, :256]
                n = h * 8 + m
                if n:
                    cosine, sine_part = cosine_ref[n : n + 1, :], sine_ref[n : n + 1, :]
                    real, imag = real * cosine - imag * sine_part, imag * cosine + real * sine_part
                values.append((real, imag))
        shift = kz + symbol_x_ref[j]
        for k, (real, imag) in enumerate(sixteen(values)):
            factor = scale / (shift + symbol_ref[k : k + 1, :])
            out_ref[0, j, :, k * 256 : (k + 1) * 256] = real * factor
            out_ref[1, j, :, k * 256 : (k + 1) * 256] = imag * factor


def y_transform(first, second, place, symbol_x, kz_square):
    table, cosine, sine_part, symbol = y_tables()
    return call(
        y_kernel,
        "y_transform",
        floats(2, 8, PLANES, LENGTH),
        [place, symbol_x],
        jnp.asarray(table),
        jnp.asarray(cosine),
        jnp.asarray(sine_part),
        jnp.asarray(symbol),
        jnp.broadcast_to(kz_square[:, None], (PLANES, 256)),
        first.reshape(8 * SLOT, LANES),
        *second,
        scratch=[pltpu.VMEM((8 * SLOT, LANES), jnp.float32)],
    )


def around(parts, axes):
    count = len(parts)
    return [
        part if step == 0 else lax.ppermute(part, axes, [(i, (i + step) % count) for i in range(count)])
        for step, part in enumerate(parts)
    ]


def across(whole, axes):
    return lax.all_to_all(whole, axes, 0, 0, tiled=True)


def body(density, kz_square):
    zh = lax.axis_index("zh")
    z = zh * 2 + lax.axis_index("zl")
    place = jnp.stack([zh, z]).astype(jnp.int32)
    *first, second = pack(density, place)
    first = around(first, "zh")
    second = split(across(second, ("x", "y")))
    first = across(join(first), ("x", "y"))
    second = around(second, "zh")
    first = x_transform_first(first, place)
    first = around(first, ("zh", "zl"))
    second = x_transform_second(second, place)
    second = split(across(second, ("x", "y", "core")))
    first = across(join(first), ("x", "y", "core"))
    second = around(second, ("zh", "zl"))
    wave_x = (lax.axis_index(AXES) * 8 + jnp.arange(8, dtype=jnp.int32)).astype(jnp.float32)
    symbol_x = 4.0 * jnp.sin(wave_x * (math.pi / LENGTH)) ** 2
    return y_transform(first, second, place, symbol_x, kz_square)


def solution(mesh):
    fine = Mesh(mesh.devices.reshape(4, 4, 4, 2, 2), AXES)
    in_specs = (P(AXES[:3], AXES[3:]), P())
    out_specs = P(None, AXES, None, None)
    return jax.shard_map(body, mesh=fine, in_specs=in_specs, out_specs=out_specs, check_vma=False)
```

```python
import functools
import math

import jax
import jax.numpy as jnp
import ml_dtypes
import numpy as np
from jax import lax
from jax.experimental import pallas as pl
from jax.experimental.pallas import tpu as pltpu
from jax.sharding import Mesh
from jax.sharding import PartitionSpec as P

LENGTH = 4096
KEPT = 2048
ROOT = 64
LANES = 128
PITCH = 72
PLANES = 8
AXES = ("zh", "x", "y", "zl", "core")


def split_table(table, axis, order):
    high = table.astype(ml_dtypes.bfloat16)
    low = (table - high.astype(np.float64)).astype(ml_dtypes.bfloat16)
    parts = {"h": high, "l": low}
    return np.concatenate([parts[name] for name in order], axis=axis)


def split_data(values, axis, order):
    high = values.astype(jnp.bfloat16)
    low = (values - high.astype(jnp.float32)).astype(jnp.bfloat16)
    parts = {"h": high, "l": low}
    return jnp.concatenate([parts[name] for name in order], axis=axis)


@functools.cache
def x_tables():
    a = np.arange(ROOT)
    first = 2.0 * np.pi * np.outer(np.arange(ROOT // 2 + 1), a) / ROOT
    outer = np.concatenate([np.cos(first), -np.sin(first[1 : ROOT // 2])], axis=0)
    sections = []
    k2 = np.arange(KEPT // ROOT)
    for k1 in range(ROOT // 2 + 1):
        rows = []
        for k in (k1, (ROOT - k1) % ROOT):
            angle = 2.0 * np.pi * np.outer(k + ROOT * k2, a) / LENGTH
            rows += [np.cos(angle), np.sin(angle)]
        sections.append(np.concatenate(rows, axis=0))
    return split_table(outer, 1, "hhl"), split_table(np.stack(sections), 2, "hhl")


@functools.cache
def y_tables():
    source = np.arange(256)
    place = (source % 4) * 64 + source // 4
    angle = 2.0 * np.pi * np.outer(place, np.arange(256)) / 256
    table = np.concatenate([np.cos(angle), -np.sin(angle)], axis=1)
    turn = 2.0 * np.pi * np.outer(np.arange(16), np.arange(256)) / LENGTH
    wave = np.arange(LENGTH).reshape(16, 256)
    symbol = 4.0 * np.sin(np.pi * wave / LENGTH) ** 2
    return (
        split_table(table, 0, "hhl"),
        np.cos(turn).astype(np.float32),
        (-np.sin(turn)).astype(np.float32),
        symbol.astype(np.float32),
    )


def x_kernel(outer_ref, section_ref, lines_ref, out_ref, mixed_ref):
    outer = outer_ref[...]
    for b in range(0, ROOT, 2):
        pair = jnp.concatenate(
            [lines_ref[pl.ds(b + i, ROOT, stride=ROOT), :] for i in range(2)], axis=1
        )
        mixed = jnp.dot(outer, split_data(pair, 0, "hlh"), preferred_element_type=jnp.float32)
        for i in range(2):
            mixed_ref[pl.ds(b + i, ROOT, stride=PITCH), :] = mixed[:, i * LANES : (i + 1) * LANES]
    count = KEPT // ROOT

    def store(k1, part, values):
        start = (k1 // 8) * 16 + part * 8 + k1 % 8
        out_ref[pl.ds(start, count, stride=LANES), :] = values

    for k1 in range(ROOT // 2 + 1):
        real = mixed_ref[k1 * PITCH : k1 * PITCH + ROOT, :]
        if 0 < k1 < ROOT // 2:
            at = (ROOT // 2 + k1) * PITCH
            values = jnp.concatenate([real, mixed_ref[at : at + ROOT, :]], axis=1)
            result = jnp.dot(section_ref[k1], split_data(values, 0, "hlh"), preferred_element_type=jnp.float32)
            cosine, sine_part = result[:count], result[count : 2 * count]
            store(k1, 0, cosine[:, :LANES] + sine_part[:, LANES:])
            store(k1, 1, cosine[:, LANES:] - sine_part[:, :LANES])
            cosine, sine_part = result[2 * count : 3 * count], result[3 * count :]
            store(ROOT - k1, 0, cosine[:, :LANES] - sine_part[:, LANES:])
            store(ROOT - k1, 1, -cosine[:, LANES:] - sine_part[:, :LANES])
        else:
            section = section_ref[k1, : 2 * count, :]
            result = jnp.dot(section, split_data(real, 0, "hlh"), preferred_element_type=jnp.float32)
            store(k1, 0, result[:count])
            store(k1, 1, -result[count:])


def x_transform(lines):
    outer, sections = x_tables()
    return pl.pallas_call(
        x_kernel,
        out_shape=jax.ShapeDtypeStruct((LENGTH, LANES), jnp.float32),
        scratch_shapes=[pltpu.VMEM((ROOT * PITCH, LANES), jnp.float32)],
        compiler_params=pltpu.CompilerParams(vmem_limit_bytes=40 << 20),
        name="x_transform",
    )(jnp.asarray(outer), jnp.asarray(sections), lines)


def add(p, q):
    return (p[0] + q[0], p[1] + q[1])


def sub(p, q):
    return (p[0] - q[0], p[1] - q[1])


def turn_back(p):
    return (p[1], -p[0])


def times(p, angle):
    cosine, sine_part = math.cos(angle), math.sin(angle)
    return (p[0] * cosine - p[1] * sine_part, p[1] * cosine + p[0] * sine_part)


def four(p, q, r, s):
    even, odd = add(p, r), add(q, s)
    even_minus, odd_minus = sub(p, r), turn_back(sub(q, s))
    return add(even, odd), add(even_minus, odd_minus), sub(even, odd), sub(even_minus, odd_minus)


def sixteen(values):
    columns = []
    for n in range(4):
        column = four(*[values[4 * m + n] for m in range(4)])
        columns.append([times(v, -2.0 * math.pi * n * k / 16) if n * k else v for k, v in enumerate(column)])
    out = [None] * 16
    for k in range(4):
        for l, v in enumerate(four(*[columns[n][k] for n in range(4)])):
            out[k + 4 * l] = v
    return out


def y_kernel(place_ref, symbol_x_ref, kz_ref, table_ref, cosine_ref, sine_ref, symbol_ref, lines_ref, out_ref, done_ref, sent):
    table = table_ref[...]
    scale = -1.0 / math.sqrt(LENGTH * LENGTH)
    row = lax.broadcasted_iota(jnp.int32, (PLANES, 256), 0)
    kz = jnp.zeros((PLANES, 256), jnp.float32)
    for p in range(PLANES):
        kz = jnp.where(row == p, kz_ref[p], kz)
    copies = []
    for j in range(8):
        rows = []
        for part in range(2):
            values = lines_ref[pl.ds(part * 8 + j, 256, stride=16), :]
            rows.append(split_data(values.T, 1, "hlh"))
        product = jnp.dot(jnp.concatenate(rows, axis=0), table, preferred_element_type=jnp.float32)
        values = []
        for n in range(16):
            first = product[n * 8 : n * 8 + 8]
            second = product[LANES + n * 8 : LANES + n * 8 + 8]
            real = first[:, :256] - second[:, 256:]
            imag = first[:, 256:] + second[:, :256]
            if n:
                cosine, sine_part = cosine_ref[n : n + 1, :], sine_ref[n : n + 1, :]
                real, imag = real * cosine - imag * sine_part, imag * cosine + real * sine_part
            values.append((real, imag))
        shift = kz + symbol_x_ref[place_ref[0] * 8 + j]
        for k, (real, imag) in enumerate(sixteen(values)):
            factor = scale / (shift + symbol_ref[k : k + 1, :])
            done_ref[j, 0, :, k * 256 : (k + 1) * 256] = real * factor
            done_ref[j, 1, :, k * 256 : (k + 1) * 256] = imag * factor
        copies.append(pltpu.make_async_copy(done_ref.at[j], out_ref.at[:, j], sent.at[j]))
        copies[-1].start()
    for copy in copies:
        copy.wait()


def y_transform(lines, place, kz_square):
    table, cosine, sine_part, symbol = y_tables()
    symbol_x = (4.0 * np.sin(np.pi * np.arange(KEPT) / LENGTH) ** 2).astype(np.float32)
    vmem = pl.BlockSpec(memory_space=pltpu.VMEM)
    smem = pl.BlockSpec(memory_space=pltpu.SMEM)
    return pl.pallas_call(
        y_kernel,
        out_shape=jax.ShapeDtypeStruct((2, 8, PLANES, LENGTH), jnp.float32),
        in_specs=[smem] * 3 + [vmem] * 5,
        out_specs=pl.BlockSpec(memory_space=pl.ANY),
        scratch_shapes=[
            pltpu.VMEM((8, 2, PLANES, LENGTH), jnp.float32),
            pltpu.SemaphoreType.DMA((8,)),
        ],
        compiler_params=pltpu.CompilerParams(vmem_limit_bytes=40 << 20),
        name="y_transform",
    )(
        place,
        jnp.asarray(symbol_x),
        kz_square,
        jnp.asarray(table),
        jnp.asarray(cosine),
        jnp.asarray(sine_part),
        jnp.asarray(symbol),
        lines,
    )


def body(density, kz_square):
    place = jnp.stack([lax.axis_index(AXES)]).astype(jnp.int32)
    blocks = jnp.transpose(density.reshape(ROOT, ROOT, LANES), (1, 0, 2))
    lines = lax.all_to_all(blocks, AXES[:3], 0, 0, tiled=True)
    spectrum = x_transform(lines.reshape(LENGTH, LANES))
    lines = lax.all_to_all(spectrum.reshape(256, 16, LANES), AXES, 0, 0, tiled=True)
    return y_transform(lines.reshape(LENGTH, LANES), place, kz_square)


def solution(mesh):
    fine = Mesh(mesh.devices.reshape(4, 4, 4, 2, 2), AXES)
    in_specs = (P(AXES[:3], AXES[3:]), P())
    out_specs = P(None, AXES, None, None)
    return jax.shard_map(body, mesh=fine, in_specs=in_specs, out_specs=out_specs, check_vma=False)
```

```python
import functools
import math

import jax
import jax.numpy as jnp
import ml_dtypes
import numpy as np
from jax import lax
from jax.experimental import pallas as pl
from jax.experimental.pallas import tpu as pltpu
from jax.sharding import Mesh
from jax.sharding import PartitionSpec as P

LENGTH = 4096
KEPT = 2048
ROOT = 64
LANES = 128
PITCH = 72
PLANES = 8
AXES = ("zh", "x", "y", "zl", "core")


def split_table(table, axis, order):
    high = table.astype(ml_dtypes.bfloat16)
    low = (table - high.astype(np.float64)).astype(ml_dtypes.bfloat16)
    parts = {"h": high, "l": low}
    return np.concatenate([parts[name] for name in order], axis=axis)


def split_data(values, axis, order):
    high = values.astype(jnp.bfloat16)
    low = (values - high.astype(jnp.float32)).astype(jnp.bfloat16)
    parts = {"h": high, "l": low}
    return jnp.concatenate([parts[name] for name in order], axis=axis)


@functools.cache
def x_tables():
    a = np.arange(ROOT)
    first = 2.0 * np.pi * np.outer(np.arange(ROOT // 2 + 1), a) / ROOT
    outer = np.concatenate([np.cos(first), -np.sin(first[1 : ROOT // 2])], axis=0)
    sections = []
    k2 = np.arange(KEPT // ROOT)
    for k1 in range(ROOT // 2 + 1):
        rows = []
        for k in (k1, (ROOT - k1) % ROOT):
            angle = 2.0 * np.pi * np.outer(k + ROOT * k2, a) / LENGTH
            rows += [np.cos(angle), np.sin(angle)]
        sections.append(np.concatenate(rows, axis=0))
    return split_table(outer, 1, "hhl"), split_table(np.stack(sections), 2, "hhl")


@functools.cache
def y_tables():
    source = np.arange(256)
    place = (source % 4) * 64 + source // 4
    angle = 2.0 * np.pi * np.outer(place, np.arange(256)) / 256
    table = np.concatenate([np.cos(angle), -np.sin(angle)], axis=1)
    turn = 2.0 * np.pi * np.outer(np.arange(16), np.arange(256)) / LENGTH
    wave = np.arange(LENGTH).reshape(16, 256)
    symbol = 4.0 * np.sin(np.pi * wave / LENGTH) ** 2
    return (
        split_table(table, 0, "hhl"),
        np.cos(turn).astype(np.float32),
        (-np.sin(turn)).astype(np.float32),
        symbol.astype(np.float32),
    )


def x_kernel(place_ref, outer_ref, section_ref, lines_ref, out_ref, mixed_ref, staged_ref):
    outer = outer_ref[...]
    for a in range(ROOT):
        staged_ref[a * PITCH : a * PITCH + ROOT, :] = lines_ref[a * ROOT : (a + 1) * ROOT, :]
    for b in range(0, ROOT, 2):
        pair = jnp.concatenate(
            [staged_ref[pl.ds(b + i, ROOT, stride=PITCH), :] for i in range(2)], axis=1
        )
        mixed = jnp.dot(outer, split_data(pair, 0, "hlh"), preferred_element_type=jnp.float32)
        for i in range(2):
            mixed_ref[pl.ds(b + i, ROOT, stride=PITCH), :] = mixed[:, i * LANES : (i + 1) * LANES]
    count = KEPT // ROOT

    def store(k1, part, values):
        staged_ref[(k1 * 2 + part) * 36 : (k1 * 2 + part) * 36 + count, :] = values

    for k1 in range(ROOT // 2 + 1):
        real = mixed_ref[k1 * PITCH : k1 * PITCH + ROOT, :]
        if 0 < k1 < ROOT // 2:
            at = (ROOT // 2 + k1) * PITCH
            values = jnp.concatenate([real, mixed_ref[at : at + ROOT, :]], axis=1)
            result = jnp.dot(section_ref[k1], split_data(values, 0, "hlh"), preferred_element_type=jnp.float32)
            cosine, sine_part = result[:count], result[count : 2 * count]
            store(k1, 0, cosine[:, :LANES] + sine_part[:, LANES:])
            store(k1, 1, cosine[:, LANES:] - sine_part[:, :LANES])
            cosine, sine_part = result[2 * count : 3 * count], result[3 * count :]
            store(ROOT - k1, 0, cosine[:, :LANES] - sine_part[:, LANES:])
            store(ROOT - k1, 1, -cosine[:, LANES:] - sine_part[:, :LANES])
        else:
            section = section_ref[k1, : 2 * count, :]
            result = jnp.dot(section, split_data(real, 0, "hlh"), preferred_element_type=jnp.float32)
            store(k1, 0, result[:count])
            store(k1, 1, -result[count:])
    for k2 in range(count):
        for high in range(8):
            for part in range(2):
                at = (k2 * 8 + high) * 16 + part * 8
                out_ref[at : at + 8, :] = staged_ref[pl.ds((high * 16 + part) * 36 + k2, 8, stride=72), :]


def x_transform(lines, place):
    outer, sections = x_tables()
    return pl.pallas_call(
        x_kernel,
        out_shape=jax.ShapeDtypeStruct((LENGTH, LANES), jnp.float32),
        in_specs=[pl.BlockSpec(memory_space=pltpu.SMEM)] + [pl.BlockSpec(memory_space=pltpu.VMEM)] * 3,
        scratch_shapes=[pltpu.VMEM((ROOT * PITCH, LANES), jnp.float32)] * 2,
        compiler_params=pltpu.CompilerParams(vmem_limit_bytes=40 << 20),
        name="x_transform",
    )(place, jnp.asarray(outer), jnp.asarray(sections), lines)


def add(p, q):
    return (p[0] + q[0], p[1] + q[1])


def sub(p, q):
    return (p[0] - q[0], p[1] - q[1])


def turn_back(p):
    return (p[1], -p[0])


def times(p, angle):
    cosine, sine_part = math.cos(angle), math.sin(angle)
    return (p[0] * cosine - p[1] * sine_part, p[1] * cosine + p[0] * sine_part)


def four(p, q, r, s):
    even, odd = add(p, r), add(q, s)
    even_minus, odd_minus = sub(p, r), turn_back(sub(q, s))
    return add(even, odd), add(even_minus, odd_minus), sub(even, odd), sub(even_minus, odd_minus)


def sixteen(values):
    columns = []
    for n in range(4):
        column = four(*[values[4 * m + n] for m in range(4)])
        columns.append([times(v, -2.0 * math.pi * n * k / 16) if n * k else v for k, v in enumerate(column)])
    out = [None] * 16
    for k in range(4):
        for l, v in enumerate(four(*[columns[n][k] for n in range(4)])):
            out[k + 4 * l] = v
    return out


def y_kernel(place_ref, symbol_x_ref, kz_ref, table_ref, cosine_ref, sine_ref, symbol_ref, lines_ref, out_ref, done_ref, staged_ref, sent):
    table = table_ref[...]
    scale = -1.0 / math.sqrt(LENGTH * LENGTH)
    row = lax.broadcasted_iota(jnp.int32, (PLANES, 256), 0)
    kz = jnp.zeros((PLANES, 256), jnp.float32)
    for p in range(PLANES):
        kz = jnp.where(row == p, kz_ref[p], kz)
    for source in range(256):
        staged_ref[source * 24 : source * 24 + 16, :] = lines_ref[source * 16 : source * 16 + 16, :]
    copies = []
    for j in range(8):
        rows = []
        for part in range(2):
            values = staged_ref[pl.ds(part * 8 + j, 256, stride=24), :]
            rows.append(split_data(values.T, 1, "hlh"))
        product = jnp.dot(jnp.concatenate(rows, axis=0), table, preferred_element_type=jnp.float32)
        values = []
        for n in range(16):
            first = product[n * 8 : n * 8 + 8]
            second = product[LANES + n * 8 : LANES + n * 8 + 8]
            real = first[:, :256] - second[:, 256:]
            imag = first[:, 256:] + second[:, :256]
            if n:
                cosine, sine_part = cosine_ref[n : n + 1, :], sine_ref[n : n + 1, :]
                real, imag = real * cosine - imag * sine_part, imag * cosine + real * sine_part
            values.append((real, imag))
        shift = kz + symbol_x_ref[place_ref[0] * 8 + j]
        for k, (real, imag) in enumerate(sixteen(values)):
            factor = scale / (shift + symbol_ref[k : k + 1, :])
            done_ref[j, 0, :, k * 256 : (k + 1) * 256] = real * factor
            done_ref[j, 1, :, k * 256 : (k + 1) * 256] = imag * factor
        copies.append(pltpu.make_async_copy(done_ref.at[j], out_ref.at[:, j], sent.at[j]))
        copies[-1].start()
    for copy in copies:
        copy.wait()


def y_transform(lines, place, kz_square):
    table, cosine, sine_part, symbol = y_tables()
    symbol_x = (4.0 * np.sin(np.pi * np.arange(KEPT) / LENGTH) ** 2).astype(np.float32)
    vmem = pl.BlockSpec(memory_space=pltpu.VMEM)
    smem = pl.BlockSpec(memory_space=pltpu.SMEM)
    return pl.pallas_call(
        y_kernel,
        out_shape=jax.ShapeDtypeStruct((2, 8, PLANES, LENGTH), jnp.float32),
        in_specs=[smem] * 3 + [vmem] * 5,
        out_specs=pl.BlockSpec(memory_space=pl.ANY),
        scratch_shapes=[
            pltpu.VMEM((8, 2, PLANES, LENGTH), jnp.float32),
            pltpu.VMEM((256 * 24, LANES), jnp.float32),
            pltpu.SemaphoreType.DMA((8,)),
        ],
        compiler_params=pltpu.CompilerParams(vmem_limit_bytes=40 << 20),
        name="y_transform",
    )(
        place,
        jnp.asarray(symbol_x),
        kz_square,
        jnp.asarray(table),
        jnp.asarray(cosine),
        jnp.asarray(sine_part),
        jnp.asarray(symbol),
        lines,
    )


def body(density, kz_square):
    place = jnp.stack([lax.axis_index(AXES)]).astype(jnp.int32)
    blocks = jnp.transpose(density.reshape(ROOT, ROOT, LANES), (1, 0, 2))
    lines = lax.all_to_all(blocks, AXES[:3], 0, 0, tiled=True)
    spectrum = x_transform(lines.reshape(LENGTH, LANES), place)
    lines = lax.all_to_all(spectrum.reshape(256, 16, LANES), AXES, 0, 0, tiled=True)
    return y_transform(lines.reshape(LENGTH, LANES), place, kz_square)


def solution(mesh):
    fine = Mesh(mesh.devices.reshape(4, 4, 4, 2, 2), AXES)
    in_specs = (P(AXES[:3], AXES[3:]), P())
    out_specs = P(None, AXES, None, None)
    return jax.shard_map(body, mesh=fine, in_specs=in_specs, out_specs=out_specs, check_vma=False)
```

```python
import functools
import math

import jax
import jax.numpy as jnp
import ml_dtypes
import numpy as np
from jax import lax
from jax.experimental import pallas as pl
from jax.experimental.pallas import tpu as pltpu
from jax.sharding import Mesh
from jax.sharding import PartitionSpec as P

LENGTH = 4096
KEPT = 2048
ROOT = 64
LANES = 128
PITCH = 72
PLANES = 8
AXES = ("zh", "x", "y", "zl", "core")
SIZES = (4, 4, 4, 2, 2)


def split_table(table, axis, order):
    high = table.astype(ml_dtypes.bfloat16)
    low = (table - high.astype(np.float64)).astype(ml_dtypes.bfloat16)
    parts = {"h": high, "l": low}
    return np.concatenate([parts[name] for name in order], axis=axis)


def split_data(values, axis, order):
    high = values.astype(jnp.bfloat16)
    low = (values - high.astype(jnp.float32)).astype(jnp.bfloat16)
    parts = {"h": high, "l": low}
    return jnp.concatenate([parts[name] for name in order], axis=axis)


@functools.cache
def x_tables():
    a = np.arange(ROOT)
    first = 2.0 * np.pi * np.outer(np.arange(ROOT // 2 + 1), a) / ROOT
    outer = np.concatenate([np.cos(first), -np.sin(first[1 : ROOT // 2])], axis=0)
    sections = []
    k2 = np.arange(KEPT // ROOT)
    for k1 in range(ROOT // 2 + 1):
        rows = []
        for k in (k1, (ROOT - k1) % ROOT):
            angle = 2.0 * np.pi * np.outer(k + ROOT * k2, a) / LENGTH
            rows += [np.cos(angle), np.sin(angle)]
        sections.append(np.concatenate(rows, axis=0))
    return split_table(outer, 1, "hhl"), split_table(np.stack(sections), 2, "hhl")


@functools.cache
def y_tables():
    source = np.arange(256)
    place = (source % 4) * 64 + source // 4
    angle = 2.0 * np.pi * np.outer(place, np.arange(256)) / 256
    table = np.concatenate([np.cos(angle), -np.sin(angle)], axis=1)
    turn = 2.0 * np.pi * np.outer(np.arange(16), np.arange(256)) / LENGTH
    wave = np.arange(LENGTH).reshape(16, 256)
    symbol = 4.0 * np.sin(np.pi * wave / LENGTH) ** 2
    return (
        split_table(table, 0, "hhl"),
        np.cos(turn).astype(np.float32),
        (-np.sin(turn)).astype(np.float32),
        symbol.astype(np.float32),
    )


def x_kernel(outer_ref, section_ref, lines_ref, out_ref, mixed_ref, staged_ref):
    outer = outer_ref[...]
    for a in range(ROOT):
        staged_ref[a * PITCH : a * PITCH + ROOT, :] = lines_ref[a * ROOT : (a + 1) * ROOT, :]
    for b in range(0, ROOT, 2):
        pair = jnp.concatenate(
            [staged_ref[pl.ds(b + i, ROOT, stride=PITCH), :] for i in range(2)], axis=1
        )
        mixed = jnp.dot(outer, split_data(pair, 0, "hlh"), preferred_element_type=jnp.float32)
        for i in range(2):
            mixed_ref[pl.ds(b + i, ROOT, stride=PITCH), :] = mixed[:, i * LANES : (i + 1) * LANES]
    count = KEPT // ROOT

    def store(k1, part, values):
        staged_ref[(k1 * 2 + part) * 36 : (k1 * 2 + part) * 36 + count, :] = values

    for k1 in range(ROOT // 2 + 1):
        real = mixed_ref[k1 * PITCH : k1 * PITCH + ROOT, :]
        if 0 < k1 < ROOT // 2:
            at = (ROOT // 2 + k1) * PITCH
            values = jnp.concatenate([real, mixed_ref[at : at + ROOT, :]], axis=1)
            result = jnp.dot(section_ref[k1], split_data(values, 0, "hlh"), preferred_element_type=jnp.float32)
            cosine, sine_part = result[:count], result[count : 2 * count]
            store(k1, 0, cosine[:, :LANES] + sine_part[:, LANES:])
            store(k1, 1, cosine[:, LANES:] - sine_part[:, :LANES])
            cosine, sine_part = result[2 * count : 3 * count], result[3 * count :]
            store(ROOT - k1, 0, cosine[:, :LANES] - sine_part[:, LANES:])
            store(ROOT - k1, 1, -cosine[:, LANES:] - sine_part[:, :LANES])
        else:
            section = section_ref[k1, : 2 * count, :]
            result = jnp.dot(section, split_data(real, 0, "hlh"), preferred_element_type=jnp.float32)
            store(k1, 0, result[:count])
            store(k1, 1, -result[count:])
    for k2 in range(count):
        for high in range(8):
            for part in range(2):
                at = (k2 * 8 + high) * 16 + part * 8
                out_ref[at : at + 8, :] = staged_ref[pl.ds((high * 16 + part) * 36 + k2, 8, stride=72), :]


def x_transform(lines):
    outer, sections = x_tables()
    return pl.pallas_call(
        x_kernel,
        out_shape=jax.ShapeDtypeStruct((LENGTH, LANES), jnp.float32),
        scratch_shapes=[pltpu.VMEM((ROOT * PITCH, LANES), jnp.float32)] * 2,
        compiler_params=pltpu.CompilerParams(vmem_limit_bytes=40 << 20),
        name="x_transform",
    )(jnp.asarray(outer), jnp.asarray(sections), lines)


def add(p, q):
    return (p[0] + q[0], p[1] + q[1])


def sub(p, q):
    return (p[0] - q[0], p[1] - q[1])


def turn_back(p):
    return (p[1], -p[0])


def times(p, angle):
    cosine, sine_part = math.cos(angle), math.sin(angle)
    return (p[0] * cosine - p[1] * sine_part, p[1] * cosine + p[0] * sine_part)


def four(p, q, r, s):
    even, odd = add(p, r), add(q, s)
    even_minus, odd_minus = sub(p, r), turn_back(sub(q, s))
    return add(even, odd), add(even_minus, odd_minus), sub(even, odd), sub(even_minus, odd_minus)


def sixteen(values):
    columns = []
    for n in range(4):
        column = four(*[values[4 * m + n] for m in range(4)])
        columns.append([times(v, -2.0 * math.pi * n * k / 16) if n * k else v for k, v in enumerate(column)])
    out = [None] * 16
    for k in range(4):
        for l, v in enumerate(four(*[columns[n][k] for n in range(4)])):
            out[k + 4 * l] = v
    return out


def y_kernel(symbol_x_ref, kz_ref, table_ref, cosine_ref, sine_ref, symbol_ref, lines_ref, out_ref, done_ref, staged_ref, sent):
    table = table_ref[...]
    scale = -1.0 / math.sqrt(LENGTH * LENGTH)
    row = lax.broadcasted_iota(jnp.int32, (PLANES, 256), 0)
    kz = jnp.zeros((PLANES, 256), jnp.float32)
    for p in range(PLANES):
        kz = jnp.where(row == p, kz_ref[p], kz)
    for source in range(256):
        staged_ref[source * 24 : source * 24 + 16, :] = lines_ref[source * 16 : source * 16 + 16, :]
    device = 0
    for axis, size in zip(AXES, SIZES):
        device = device * size + lax.axis_index(axis)
    copies = []
    for j in range(8):
        rows = []
        for part in range(2):
            values = staged_ref[pl.ds(part * 8 + j, 256, stride=24), :]
            rows.append(split_data(values.T, 1, "hlh"))
        product = jnp.dot(jnp.concatenate(rows, axis=0), table, preferred_element_type=jnp.float32)
        values = []
        for n in range(16):
            first = product[n * 8 : n * 8 + 8]
            second = product[LANES + n * 8 : LANES + n * 8 + 8]
            real = first[:, :256] - second[:, 256:]
            imag = first[:, 256:] + second[:, :256]
            if n:
                cosine, sine_part = cosine_ref[n : n + 1, :], sine_ref[n : n + 1, :]
                real, imag = real * cosine - imag * sine_part, imag * cosine + real * sine_part
            values.append((real, imag))
        shift = kz + symbol_x_ref[device * 8 + j]
        for k, (real, imag) in enumerate(sixteen(values)):
            factor = scale / (shift + symbol_ref[k : k + 1, :])
            done_ref[j, 0, :, k * 256 : (k + 1) * 256] = real * factor
            done_ref[j, 1, :, k * 256 : (k + 1) * 256] = imag * factor
        copies.append(pltpu.make_async_copy(done_ref.at[j], out_ref.at[:, j], sent.at[j]))
        copies[-1].start()
    for copy in copies:
        copy.wait()


def y_transform(lines, kz_square):
    table, cosine, sine_part, symbol = y_tables()
    symbol_x = (4.0 * np.sin(np.pi * np.arange(KEPT) / LENGTH) ** 2).astype(np.float32)
    vmem = pl.BlockSpec(memory_space=pltpu.VMEM)
    smem = pl.BlockSpec(memory_space=pltpu.SMEM)
    return pl.pallas_call(
        y_kernel,
        out_shape=jax.ShapeDtypeStruct((2, 8, PLANES, LENGTH), jnp.float32),
        in_specs=[smem] * 2 + [vmem] * 5,
        out_specs=pl.BlockSpec(memory_space=pl.ANY),
        scratch_shapes=[
            pltpu.VMEM((8, 2, PLANES, LENGTH), jnp.float32),
            pltpu.VMEM((256 * 24, LANES), jnp.float32),
            pltpu.SemaphoreType.DMA((8,)),
        ],
        compiler_params=pltpu.CompilerParams(vmem_limit_bytes=40 << 20),
        name="y_transform",
    )(
        jnp.asarray(symbol_x),
        kz_square,
        jnp.asarray(table),
        jnp.asarray(cosine),
        jnp.asarray(sine_part),
        jnp.asarray(symbol),
        lines,
    )


def body(density, kz_square):
    blocks = jnp.transpose(density.reshape(ROOT, ROOT, LANES), (1, 0, 2))
    lines = lax.all_to_all(blocks, AXES[:3], 0, 0, tiled=True)
    spectrum = x_transform(lines.reshape(LENGTH, LANES))
    lines = lax.all_to_all(spectrum.reshape(256, 16, LANES), AXES, 0, 0, tiled=True)
    return y_transform(lines.reshape(LENGTH, LANES), kz_square)


def solution(mesh):
    fine = Mesh(mesh.devices.reshape(SIZES), AXES)
    in_specs = (P(AXES[:3], AXES[3:]), P())
    out_specs = P(None, AXES, None, None)
    return jax.shard_map(body, mesh=fine, in_specs=in_specs, out_specs=out_specs, check_vma=False)
```

```python
import functools
import math

import jax
import jax.numpy as jnp
import ml_dtypes
import numpy as np
from jax import lax
from jax.experimental import pallas as pl
from jax.experimental.pallas import tpu as pltpu
from jax.sharding import Mesh
from jax.sharding import PartitionSpec as P

LENGTH = 4096
KEPT = 2048
ROOT = 64
LANES = 128
PITCH = 72
ROWS = 32
PLANES = 8
AXES = ("zh", "x", "y", "zl", "core")
SIZES = (4, 4, 4, 2, 2)
LIMIT = pltpu.CompilerParams(vmem_limit_bytes=24 << 20)


def split_table(table, axis, order):
    high = table.astype(ml_dtypes.bfloat16)
    low = (table - high.astype(np.float64)).astype(ml_dtypes.bfloat16)
    parts = {"h": high, "l": low}
    return np.concatenate([parts[name] for name in order], axis=axis)


def split_data(values, axis, order):
    high = values.astype(jnp.bfloat16)
    low = (values - high.astype(jnp.float32)).astype(jnp.bfloat16)
    parts = {"h": high, "l": low}
    return jnp.concatenate([parts[name] for name in order], axis=axis)


@functools.cache
def x_tables():
    a = np.arange(ROOT)
    first = 2.0 * np.pi * np.outer(np.arange(ROOT // 2 + 1), a) / ROOT
    outer = np.concatenate([np.cos(first), -np.sin(first[1 : ROOT // 2])], axis=0)
    sections = []
    k2 = np.arange(KEPT // ROOT)
    for k1 in range(ROOT // 2 + 1):
        rows = []
        for k in (k1, (ROOT - k1) % ROOT):
            angle = 2.0 * np.pi * np.outer(k + ROOT * k2, a) / LENGTH
            rows += [np.cos(angle), np.sin(angle)]
        sections.append(np.concatenate(rows, axis=0))
    return split_table(outer, 1, "hhl"), split_table(np.stack(sections), 2, "hhl")


@functools.cache
def y_tables():
    source = np.arange(256)
    place = (source % 4) * 64 + source // 4
    angle = 2.0 * np.pi * np.outer(place, np.arange(256)) / 256
    table = np.concatenate([np.cos(angle), -np.sin(angle)], axis=1)
    turn = 2.0 * np.pi * np.outer(np.arange(16), np.arange(256)) / LENGTH
    wave = np.arange(LENGTH).reshape(16, 256)
    symbol = 4.0 * np.sin(np.pi * wave / LENGTH) ** 2
    return (
        split_table(table, 0, "hhl"),
        np.cos(turn).astype(np.float32),
        (-np.sin(turn)).astype(np.float32),
        symbol.astype(np.float32),
    )


def pack_kernel(density_ref, *out_refs):
    zh = lax.axis_index("zh")
    for dz in range(4):
        base = ((zh + dz) & 3) * (16 * LANES)
        for xy in range(16):
            columns = pl.ds(pl.multiple_of(base + xy * LANES, LANES), LANES)
            out_refs[dz][xy] = density_ref[:ROWS, columns]
            out_refs[4][xy, dz] = density_ref[ROWS:, columns]


def join_kernel(earlier_ref, *refs):
    for slot, ref in enumerate(refs[:-1]):
        refs[-1][:, slot] = ref[...]


def split_kernel(in_ref, *out_refs):
    for slot, ref in enumerate(out_refs):
        ref[...] = in_ref[:, slot]


def floats(*shape):
    return pltpu.VMEM(shape, jnp.float32)


def pack(density):
    out_shape = [floats(16, ROWS, LANES)] * 4 + [floats(16, 4, ROWS, LANES)]
    return pl.pallas_call(pack_kernel, out_shape=out_shape, name="pack", compiler_params=LIMIT)(density)


def join(parts, earlier):
    in_specs = [pl.BlockSpec(memory_space=pl.ANY)] + [pl.BlockSpec(memory_space=pltpu.VMEM)] * 4
    return pl.pallas_call(
        join_kernel, out_shape=floats(16, 4, ROWS, LANES), in_specs=in_specs, name="join", compiler_params=LIMIT
    )(earlier, *parts)


def split(whole):
    return pl.pallas_call(
        split_kernel, out_shape=[floats(16, ROWS, LANES)] * 4, name="split", compiler_params=LIMIT
    )(whole)


def x_kernel(outer_ref, section_ref, first_ref, *refs):
    second_refs, (out_ref, mixed_ref, staged_ref) = refs[:4], refs[4:]
    outer = outer_ref[...]
    zh = lax.axis_index("zh")
    for dz in range(4):
        base = ((zh - dz) & 3) * (16 * PITCH)
        for xy in range(16):
            start = pl.multiple_of(base + xy * PITCH, 8)
            staged_ref[pl.ds(start, ROWS), :] = first_ref[xy, dz]
            staged_ref[pl.ds(start + ROWS, ROWS), :] = second_refs[dz][xy]
    for b in range(0, ROOT, 2):
        pair = jnp.concatenate(
            [staged_ref[pl.ds(b + i, ROOT, stride=PITCH), :] for i in range(2)], axis=1
        )
        mixed = jnp.dot(outer, split_data(pair, 0, "hlh"), preferred_element_type=jnp.float32)
        for i in range(2):
            mixed_ref[pl.ds(b + i, ROOT, stride=PITCH), :] = mixed[:, i * LANES : (i + 1) * LANES]
    count = KEPT // ROOT

    def store(k1, part, values):
        staged_ref[(k1 * 2 + part) * 36 : (k1 * 2 + part) * 36 + count, :] = values

    for k1 in range(ROOT // 2 + 1):
        real = mixed_ref[k1 * PITCH : k1 * PITCH + ROOT, :]
        if 0 < k1 < ROOT // 2:
            at = (ROOT // 2 + k1) * PITCH
            values = jnp.concatenate([real, mixed_ref[at : at + ROOT, :]], axis=1)
            result = jnp.dot(section_ref[k1], split_data(values, 0, "hlh"), preferred_element_type=jnp.float32)
            cosine, sine_part = result[:count], result[count : 2 * count]
            store(k1, 0, cosine[:, :LANES] + sine_part[:, LANES:])
            store(k1, 1, cosine[:, LANES:] - sine_part[:, :LANES])
            cosine, sine_part = result[2 * count : 3 * count], result[3 * count :]
            store(ROOT - k1, 0, cosine[:, :LANES] - sine_part[:, LANES:])
            store(ROOT - k1, 1, -cosine[:, LANES:] - sine_part[:, :LANES])
        else:
            section = section_ref[k1, : 2 * count, :]
            result = jnp.dot(section, split_data(real, 0, "hlh"), preferred_element_type=jnp.float32)
            store(k1, 0, result[:count])
            store(k1, 1, -result[count:])
    for k2 in range(count):
        for high in range(8):
            for part in range(2):
                at = (k2 * 8 + high) * 16 + part * 8
                out_ref[at : at + 8, :] = staged_ref[pl.ds((high * 16 + part) * 36 + k2, 8, stride=72), :]


def x_transform(first, second):
    outer, sections = x_tables()
    return pl.pallas_call(
        x_kernel,
        out_shape=jax.ShapeDtypeStruct((LENGTH, LANES), jnp.float32),
        scratch_shapes=[pltpu.VMEM((ROOT * PITCH, LANES), jnp.float32)] * 2,
        compiler_params=LIMIT,
        name="x_transform",
    )(jnp.asarray(outer), jnp.asarray(sections), first, *second)


def add(p, q):
    return (p[0] + q[0], p[1] + q[1])


def sub(p, q):
    return (p[0] - q[0], p[1] - q[1])


def turn_back(p):
    return (p[1], -p[0])


def times(p, angle):
    cosine, sine_part = math.cos(angle), math.sin(angle)
    return (p[0] * cosine - p[1] * sine_part, p[1] * cosine + p[0] * sine_part)


def four(p, q, r, s):
    even, odd = add(p, r), add(q, s)
    even_minus, odd_minus = sub(p, r), turn_back(sub(q, s))
    return add(even, odd), add(even_minus, odd_minus), sub(even, odd), sub(even_minus, odd_minus)


def sixteen(values):
    columns = []
    for n in range(4):
        column = four(*[values[4 * m + n] for m in range(4)])
        columns.append([times(v, -2.0 * math.pi * n * k / 16) if n * k else v for k, v in enumerate(column)])
    out = [None] * 16
    for k in range(4):
        for l, v in enumerate(four(*[columns[n][k] for n in range(4)])):
            out[k + 4 * l] = v
    return out


def y_kernel(symbol_x_ref, kz_ref, table_ref, cosine_ref, sine_ref, symbol_ref, lines_ref, out_ref, done_ref, staged_ref, sent):
    table = table_ref[...]
    scale = -1.0 / math.sqrt(LENGTH * LENGTH)
    row = lax.broadcasted_iota(jnp.int32, (PLANES, 256), 0)
    kz = jnp.zeros((PLANES, 256), jnp.float32)
    for p in range(PLANES):
        kz = jnp.where(row == p, kz_ref[p], kz)
    for source in range(256):
        staged_ref[source * 24 : source * 24 + 16, :] = lines_ref[source * 16 : source * 16 + 16, :]
    device = 0
    for axis, size in zip(AXES, SIZES):
        device = device * size + lax.axis_index(axis)
    copies = []
    for j in range(8):
        rows = []
        for part in range(2):
            values = staged_ref[pl.ds(part * 8 + j, 256, stride=24), :]
            rows.append(split_data(values.T, 1, "hlh"))
        product = jnp.dot(jnp.concatenate(rows, axis=0), table, preferred_element_type=jnp.float32)
        values = []
        for n in range(16):
            first = product[n * 8 : n * 8 + 8]
            second = product[LANES + n * 8 : LANES + n * 8 + 8]
            real = first[:, :256] - second[:, 256:]
            imag = first[:, 256:] + second[:, :256]
            if n:
                cosine, sine_part = cosine_ref[n : n + 1, :], sine_ref[n : n + 1, :]
                real, imag = real * cosine - imag * sine_part, imag * cosine + real * sine_part
            values.append((real, imag))
        shift = kz + symbol_x_ref[device * 8 + j]
        for k, (real, imag) in enumerate(sixteen(values)):
            factor = scale / (shift + symbol_ref[k : k + 1, :])
            done_ref[j, 0, :, k * 256 : (k + 1) * 256] = real * factor
            done_ref[j, 1, :, k * 256 : (k + 1) * 256] = imag * factor
        copies.append(pltpu.make_async_copy(done_ref.at[j], out_ref.at[:, j], sent.at[j]))
        copies[-1].start()
    for copy in copies:
        copy.wait()


def y_transform(lines, kz_square):
    table, cosine, sine_part, symbol = y_tables()
    symbol_x = (4.0 * np.sin(np.pi * np.arange(KEPT) / LENGTH) ** 2).astype(np.float32)
    vmem = pl.BlockSpec(memory_space=pltpu.VMEM)
    smem = pl.BlockSpec(memory_space=pltpu.SMEM)
    return pl.pallas_call(
        y_kernel,
        out_shape=jax.ShapeDtypeStruct((2, 8, PLANES, LENGTH), jnp.float32),
        in_specs=[smem] * 2 + [vmem] * 5,
        out_specs=pl.BlockSpec(memory_space=pl.ANY),
        scratch_shapes=[
            pltpu.VMEM((8, 2, PLANES, LENGTH), jnp.float32),
            pltpu.VMEM((256 * 24, LANES), jnp.float32),
            pltpu.SemaphoreType.DMA((8,)),
        ],
        compiler_params=LIMIT,
        name="y_transform",
    )(
        jnp.asarray(symbol_x),
        kz_square,
        jnp.asarray(table),
        jnp.asarray(cosine),
        jnp.asarray(sine_part),
        jnp.asarray(symbol),
        lines,
    )


def around(parts):
    arrived = list(parts)
    for dz in (2, 1, 3):
        arrived[dz] = lax.ppermute(parts[dz], "zh", [(i, (i + dz) % 4) for i in range(4)])
    return arrived


def across(whole):
    inside = lax.axis_index("core") < SIZES[4]
    return lax.cond(inside, lambda v: lax.all_to_all(v, ("x", "y"), 0, 0, tiled=True), lambda v: v, whole)


def body(density, kz_square):
    *first, second = pack(density)
    first = around(first)
    second = split(across(second))
    first = across(join(first, second[0]))
    second = around(second)
    spectrum = x_transform(first, second)
    lines = lax.all_to_all(spectrum.reshape(256, 16, LANES), AXES, 0, 0, tiled=True)
    return y_transform(lines.reshape(LENGTH, LANES), kz_square)


def solution(mesh):
    fine = Mesh(mesh.devices.reshape(SIZES), AXES)
    in_specs = (P(AXES[:3], AXES[3:]), P())
    out_specs = P(None, AXES, None, None)
    return jax.shard_map(body, mesh=fine, in_specs=in_specs, out_specs=out_specs, check_vma=False)
```

```python
import functools
import math

import jax
import jax.numpy as jnp
import ml_dtypes
import numpy as np
from jax import lax
from jax.experimental import pallas as pl
from jax.experimental.pallas import tpu as pltpu
from jax.sharding import Mesh
from jax.sharding import PartitionSpec as P

LENGTH = 4096
KEPT = 2048
ROOT = 64
LANES = 128
PITCH = 72
ROWS = 32
PLANES = 8
AXES = ("zh", "x", "y", "zl", "core")
SIZES = (4, 4, 4, 2, 2)
LIMIT = pltpu.CompilerParams(vmem_limit_bytes=24 << 20)


def split_table(table, axis, order):
    high = table.astype(ml_dtypes.bfloat16)
    low = (table - high.astype(np.float64)).astype(ml_dtypes.bfloat16)
    parts = {"h": high, "l": low}
    return np.concatenate([parts[name] for name in order], axis=axis)


def split_data(values, axis, order):
    high = values.astype(jnp.bfloat16)
    low = (values - high.astype(jnp.float32)).astype(jnp.bfloat16)
    parts = {"h": high, "l": low}
    return jnp.concatenate([parts[name] for name in order], axis=axis)


@functools.cache
def x_tables():
    a = np.arange(ROOT)
    first = 2.0 * np.pi * np.outer(np.arange(ROOT // 2 + 1), a) / ROOT
    outer = np.concatenate([np.cos(first), -np.sin(first[1 : ROOT // 2])], axis=0)
    sections = []
    k2 = np.arange(KEPT // ROOT)
    for k1 in range(ROOT // 2 + 1):
        rows = []
        for k in (k1, (ROOT - k1) % ROOT):
            angle = 2.0 * np.pi * np.outer(k + ROOT * k2, a) / LENGTH
            rows += [np.cos(angle), np.sin(angle)]
        sections.append(np.concatenate(rows, axis=0))
    return split_table(outer, 1, "hhl"), split_table(np.stack(sections), 2, "hhl")


@functools.cache
def y_tables():
    source = np.arange(256)
    place = (source % 4) * 64 + source // 4
    angle = 2.0 * np.pi * np.outer(place, np.arange(256)) / 256
    table = np.concatenate([np.cos(angle), -np.sin(angle)], axis=1)
    turn = 2.0 * np.pi * np.outer(np.arange(16), np.arange(256)) / LENGTH
    wave = np.arange(LENGTH).reshape(16, 256)
    symbol = 4.0 * np.sin(np.pi * wave / LENGTH) ** 2
    return (
        split_table(table, 0, "hhl"),
        np.cos(turn).astype(np.float32),
        (-np.sin(turn)).astype(np.float32),
        symbol.astype(np.float32),
    )


def pack_kernel(density_ref, *out_refs):
    zh = lax.axis_index("zh")
    for dz in range(4):
        base = ((zh + dz) & 3) * (16 * LANES)
        for xy in range(16):
            columns = pl.ds(pl.multiple_of(base + xy * LANES, LANES), LANES)
            out_refs[dz][xy] = density_ref[:ROWS, columns]
            out_refs[4][xy, dz] = density_ref[ROWS:, columns]


def join_kernel(earlier_ref, *refs):
    for slot, ref in enumerate(refs[:-1]):
        refs[-1][:, slot] = ref[...]


def split_kernel(in_ref, *out_refs):
    for slot, ref in enumerate(out_refs):
        ref[...] = in_ref[:, slot]


def floats(*shape):
    return pltpu.VMEM(shape, jnp.float32)


def pack(density):
    out_shape = [floats(16, ROWS, LANES)] * 4 + [floats(16, 4, ROWS, LANES)]
    return pl.pallas_call(pack_kernel, out_shape=out_shape, name="pack", compiler_params=LIMIT)(density)


def join(parts, earlier):
    in_specs = [pl.BlockSpec(memory_space=pl.ANY)] + [pl.BlockSpec(memory_space=pltpu.VMEM)] * 4
    return pl.pallas_call(
        join_kernel, out_shape=floats(16, 4, ROWS, LANES), in_specs=in_specs, name="join", compiler_params=LIMIT
    )(earlier, *parts)


def split(whole):
    return pl.pallas_call(
        split_kernel, out_shape=[floats(16, ROWS, LANES)] * 4, name="split", compiler_params=LIMIT
    )(whole)


def x_kernel(outer_ref, section_ref, first_ref, *refs):
    second_refs, (out_ref, mixed_ref, places_ref, arrived) = refs[:4], refs[4:]
    staged_ref = places_ref.reshape(ROOT * PITCH, LANES)
    outer = outer_ref[...]
    zh = lax.axis_index("zh")
    copies = []
    for dz in range(4):
        place = places_ref.at[pl.ds(((zh - dz) & 3) * 16, 16), pl.ds(ROWS, ROWS), :]
        copies.append(pltpu.make_async_copy(second_refs[dz], place, arrived.at[dz]))
        copies[-1].start()
    for dz in range(4):
        for xy in range(16):
            places_ref[((zh - dz) & 3) * 16 + xy, :ROWS, :] = first_ref[xy, dz]
    for b in range(0, ROOT, 2):
        if b == ROWS:
            for copy in copies:
                copy.wait()
        pair = jnp.concatenate(
            [staged_ref[pl.ds(b + i, ROOT, stride=PITCH), :] for i in range(2)], axis=1
        )
        mixed = jnp.dot(outer, split_data(pair, 0, "hlh"), preferred_element_type=jnp.float32)
        for i in range(2):
            mixed_ref[pl.ds(b + i, ROOT, stride=PITCH), :] = mixed[:, i * LANES : (i + 1) * LANES]
    count = KEPT // ROOT

    def store(k1, part, values):
        staged_ref[(k1 * 2 + part) * 36 : (k1 * 2 + part) * 36 + count, :] = values

    for k1 in range(ROOT // 2 + 1):
        real = mixed_ref[k1 * PITCH : k1 * PITCH + ROOT, :]
        if 0 < k1 < ROOT // 2:
            at = (ROOT // 2 + k1) * PITCH
            values = jnp.concatenate([real, mixed_ref[at : at + ROOT, :]], axis=1)
            result = jnp.dot(section_ref[k1], split_data(values, 0, "hlh"), preferred_element_type=jnp.float32)
            cosine, sine_part = result[:count], result[count : 2 * count]
            store(k1, 0, cosine[:, :LANES] + sine_part[:, LANES:])
            store(k1, 1, cosine[:, LANES:] - sine_part[:, :LANES])
            cosine, sine_part = result[2 * count : 3 * count], result[3 * count :]
            store(ROOT - k1, 0, cosine[:, :LANES] - sine_part[:, LANES:])
            store(ROOT - k1, 1, -cosine[:, LANES:] - sine_part[:, :LANES])
        else:
            section = section_ref[k1, : 2 * count, :]
            result = jnp.dot(section, split_data(real, 0, "hlh"), preferred_element_type=jnp.float32)
            store(k1, 0, result[:count])
            store(k1, 1, -result[count:])
    for k2 in range(count):
        for high in range(8):
            for part in range(2):
                at = (k2 * 8 + high) * 16 + part * 8
                out_ref[at : at + 8, :] = staged_ref[pl.ds((high * 16 + part) * 36 + k2, 8, stride=72), :]


def x_transform(first, second):
    outer, sections = x_tables()
    vmem, whole = pl.BlockSpec(memory_space=pltpu.VMEM), pl.BlockSpec(memory_space=pl.ANY)
    return pl.pallas_call(
        x_kernel,
        out_shape=jax.ShapeDtypeStruct((LENGTH, LANES), jnp.float32),
        in_specs=[vmem] * 3 + [whole] * 4,
        scratch_shapes=[
            pltpu.VMEM((ROOT * PITCH, LANES), jnp.float32),
            pltpu.VMEM((ROOT, PITCH, LANES), jnp.float32),
            pltpu.SemaphoreType.DMA((4,)),
        ],
        compiler_params=LIMIT,
        name="x_transform",
    )(jnp.asarray(outer), jnp.asarray(sections), first, *second)


def add(p, q):
    return (p[0] + q[0], p[1] + q[1])


def sub(p, q):
    return (p[0] - q[0], p[1] - q[1])


def turn_back(p):
    return (p[1], -p[0])


def times(p, angle):
    cosine, sine_part = math.cos(angle), math.sin(angle)
    return (p[0] * cosine - p[1] * sine_part, p[1] * cosine + p[0] * sine_part)


def four(p, q, r, s):
    even, odd = add(p, r), add(q, s)
    even_minus, odd_minus = sub(p, r), turn_back(sub(q, s))
    return add(even, odd), add(even_minus, odd_minus), sub(even, odd), sub(even_minus, odd_minus)


def sixteen(values):
    columns = []
    for n in range(4):
        column = four(*[values[4 * m + n] for m in range(4)])
        columns.append([times(v, -2.0 * math.pi * n * k / 16) if n * k else v for k, v in enumerate(column)])
    out = [None] * 16
    for k in range(4):
        for l, v in enumerate(four(*[columns[n][k] for n in range(4)])):
            out[k + 4 * l] = v
    return out


def y_kernel(symbol_x_ref, kz_ref, table_ref, cosine_ref, sine_ref, symbol_ref, lines_ref, out_ref, done_ref, staged_ref, sent):
    table = table_ref[...]
    scale = -1.0 / math.sqrt(LENGTH * LENGTH)
    row = lax.broadcasted_iota(jnp.int32, (PLANES, 256), 0)
    kz = jnp.zeros((PLANES, 256), jnp.float32)
    for p in range(PLANES):
        kz = jnp.where(row == p, kz_ref[p], kz)
    for source in range(256):
        staged_ref[source * 24 : source * 24 + 16, :] = lines_ref[source * 16 : source * 16 + 16, :]
    device = 0
    for axis, size in zip(AXES, SIZES):
        device = device * size + lax.axis_index(axis)
    copies = []
    for j in range(8):
        rows = []
        for part in range(2):
            values = staged_ref[pl.ds(part * 8 + j, 256, stride=24), :]
            rows.append(split_data(values.T, 1, "hlh"))
        product = jnp.dot(jnp.concatenate(rows, axis=0), table, preferred_element_type=jnp.float32)
        values = []
        for n in range(16):
            first = product[n * 8 : n * 8 + 8]
            second = product[LANES + n * 8 : LANES + n * 8 + 8]
            real = first[:, :256] - second[:, 256:]
            imag = first[:, 256:] + second[:, :256]
            if n:
                cosine, sine_part = cosine_ref[n : n + 1, :], sine_ref[n : n + 1, :]
                real, imag = real * cosine - imag * sine_part, imag * cosine + real * sine_part
            values.append((real, imag))
        shift = kz + symbol_x_ref[device * 8 + j]
        for k, (real, imag) in enumerate(sixteen(values)):
            factor = scale / (shift + symbol_ref[k : k + 1, :])
            done_ref[j, 0, :, k * 256 : (k + 1) * 256] = real * factor
            done_ref[j, 1, :, k * 256 : (k + 1) * 256] = imag * factor
        copies.append(pltpu.make_async_copy(done_ref.at[j], out_ref.at[:, j], sent.at[j]))
        copies[-1].start()
    for copy in copies:
        copy.wait()


def y_transform(lines, kz_square):
    table, cosine, sine_part, symbol = y_tables()
    symbol_x = (4.0 * np.sin(np.pi * np.arange(KEPT) / LENGTH) ** 2).astype(np.float32)
    vmem = pl.BlockSpec(memory_space=pltpu.VMEM)
    smem = pl.BlockSpec(memory_space=pltpu.SMEM)
    return pl.pallas_call(
        y_kernel,
        out_shape=jax.ShapeDtypeStruct((2, 8, PLANES, LENGTH), jnp.float32),
        in_specs=[smem] * 2 + [vmem] * 5,
        out_specs=pl.BlockSpec(memory_space=pl.ANY),
        scratch_shapes=[
            pltpu.VMEM((8, 2, PLANES, LENGTH), jnp.float32),
            pltpu.VMEM((256 * 24, LANES), jnp.float32),
            pltpu.SemaphoreType.DMA((8,)),
        ],
        compiler_params=LIMIT,
        name="y_transform",
    )(
        jnp.asarray(symbol_x),
        kz_square,
        jnp.asarray(table),
        jnp.asarray(cosine),
        jnp.asarray(sine_part),
        jnp.asarray(symbol),
        lines,
    )


def around(parts):
    arrived = list(parts)
    for dz in (2, 1, 3):
        arrived[dz] = lax.ppermute(parts[dz], "zh", [(i, (i + dz) % 4) for i in range(4)])
    return arrived


def across(whole):
    inside = lax.axis_index("core") < SIZES[4]
    return lax.cond(inside, lambda v: lax.all_to_all(v, ("x", "y"), 0, 0, tiled=True), lambda v: v, whole)


def body(density, kz_square):
    *first, second = pack(density)
    first = around(first)
    second = split(across(second))
    first = across(join(first, second[0]))
    second = around(second)
    spectrum = x_transform(first, second)
    lines = lax.all_to_all(spectrum.reshape(256, 16, LANES), AXES, 0, 0, tiled=True)
    return y_transform(lines.reshape(LENGTH, LANES), kz_square)


def solution(mesh):
    fine = Mesh(mesh.devices.reshape(SIZES), AXES)
    in_specs = (P(AXES[:3], AXES[3:]), P())
    out_specs = P(None, AXES, None, None)
    return jax.shard_map(body, mesh=fine, in_specs=in_specs, out_specs=out_specs, check_vma=False)
```

```python
import functools
import math

import jax
import jax.numpy as jnp
import ml_dtypes
import numpy as np
from jax import lax
from jax.experimental import pallas as pl
from jax.experimental.pallas import tpu as pltpu
from jax.sharding import Mesh
from jax.sharding import PartitionSpec as P

LENGTH = 4096
KEPT = 2048
ROOT = 64
LANES = 128
PITCH = 72
ROWS = 32
PLANES = 8
AXES = ("zh", "x", "y", "zl", "core")
SIZES = (4, 4, 4, 2, 2)
LIMIT = pltpu.CompilerParams(vmem_limit_bytes=24 << 20)


def split_table(table, axis, order):
    high = table.astype(ml_dtypes.bfloat16)
    low = (table - high.astype(np.float64)).astype(ml_dtypes.bfloat16)
    parts = {"h": high, "l": low}
    return np.concatenate([parts[name] for name in order], axis=axis)


def split_data(values, axis, order):
    high = values.astype(jnp.bfloat16)
    low = (values - high.astype(jnp.float32)).astype(jnp.bfloat16)
    parts = {"h": high, "l": low}
    return jnp.concatenate([parts[name] for name in order], axis=axis)


@functools.cache
def x_tables():
    a = np.arange(ROOT)
    first = 2.0 * np.pi * np.outer(np.arange(ROOT // 2 + 1), a) / ROOT
    outer = np.concatenate([np.cos(first), -np.sin(first[1 : ROOT // 2])], axis=0)
    sections = []
    k2 = np.arange(KEPT // ROOT)
    for k1 in range(ROOT // 2 + 1):
        rows = []
        for k in (k1, (ROOT - k1) % ROOT):
            angle = 2.0 * np.pi * np.outer(k + ROOT * k2, a) / LENGTH
            rows += [np.cos(angle), np.sin(angle)]
        sections.append(np.concatenate(rows, axis=0))
    return split_table(outer, 1, "hhl"), split_table(np.stack(sections), 2, "hhl")


@functools.cache
def y_tables():
    source = np.arange(256)
    place = (source % 4) * 64 + source // 4
    tables = []
    for odd in range(2):
        angle = 2.0 * np.pi * np.outer(place[place % 2 == odd], np.arange(LANES)) / 256
        tables.append(split_table(np.concatenate([np.cos(angle), -np.sin(angle)], axis=1), 0, "hhl"))
    turn = 2.0 * np.pi * np.outer(np.arange(16), np.arange(256)) / LENGTH
    wave = np.arange(LENGTH).reshape(16, 256)
    symbol = 4.0 * np.sin(np.pi * wave / LENGTH) ** 2
    return (
        np.stack(tables),
        np.cos(turn).astype(np.float32),
        (-np.sin(turn)).astype(np.float32),
        symbol.astype(np.float32),
    )


def pack_kernel(density_ref, *out_refs):
    zh = lax.axis_index("zh")
    for dz in range(4):
        base = ((zh + dz) & 3) * (16 * LANES)
        for xy in range(16):
            columns = pl.ds(pl.multiple_of(base + xy * LANES, LANES), LANES)
            out_refs[dz][xy] = density_ref[:ROWS, columns]
            out_refs[4][xy, dz] = density_ref[ROWS:, columns]


def join_kernel(earlier_ref, *refs):
    for slot, ref in enumerate(refs[:-1]):
        refs[-1][:, slot] = ref[...]


def split_kernel(in_ref, *out_refs):
    for slot, ref in enumerate(out_refs):
        ref[...] = in_ref[:, slot]


def floats(*shape):
    return pltpu.VMEM(shape, jnp.float32)


def pack(density):
    out_shape = [floats(16, ROWS, LANES)] * 4 + [floats(16, 4, ROWS, LANES)]
    return pl.pallas_call(pack_kernel, out_shape=out_shape, name="pack", compiler_params=LIMIT)(density)


def join(parts, earlier):
    in_specs = [pl.BlockSpec(memory_space=pl.ANY)] + [pl.BlockSpec(memory_space=pltpu.VMEM)] * 4
    return pl.pallas_call(
        join_kernel, out_shape=floats(16, 4, ROWS, LANES), in_specs=in_specs, name="join", compiler_params=LIMIT
    )(earlier, *parts)


def split(whole):
    return pl.pallas_call(
        split_kernel, out_shape=[floats(16, ROWS, LANES)] * 4, name="split", compiler_params=LIMIT
    )(whole)


def x_kernel(outer_ref, section_ref, first_ref, *refs):
    second_refs, (out_ref, mixed_ref, places_ref, arrived) = refs[:4], refs[4:]
    staged_ref = places_ref.reshape(ROOT * PITCH, LANES)
    outer = outer_ref[...]
    zh = lax.axis_index("zh")
    copies = []
    for dz in range(4):
        place = places_ref.at[pl.ds(((zh - dz) & 3) * 16, 16), pl.ds(ROWS, ROWS), :]
        copies.append(pltpu.make_async_copy(second_refs[dz], place, arrived.at[dz]))
        copies[-1].start()
    for dz in range(4):
        for xy in range(16):
            places_ref[((zh - dz) & 3) * 16 + xy, :ROWS, :] = first_ref[xy, dz]
    for b in range(0, ROOT, 2):
        if b == ROWS:
            for copy in copies:
                copy.wait()
        pair = jnp.concatenate(
            [staged_ref[pl.ds(b + i, ROOT, stride=PITCH), :] for i in range(2)], axis=1
        )
        mixed = jnp.dot(outer, split_data(pair, 0, "hlh"), preferred_element_type=jnp.float32)
        for i in range(2):
            mixed_ref[pl.ds(b + i, ROOT, stride=PITCH), :] = mixed[:, i * LANES : (i + 1) * LANES]
    count = KEPT // ROOT

    def store(k1, part, values):
        staged_ref[(k1 * 2 + part) * 36 : (k1 * 2 + part) * 36 + count, :] = values

    for k1 in range(ROOT // 2 + 1):
        real = mixed_ref[k1 * PITCH : k1 * PITCH + ROOT, :]
        if 0 < k1 < ROOT // 2:
            at = (ROOT // 2 + k1) * PITCH
            values = jnp.concatenate([real, mixed_ref[at : at + ROOT, :]], axis=1)
            result = jnp.dot(section_ref[k1], split_data(values, 0, "hlh"), preferred_element_type=jnp.float32)
            cosine, sine_part = result[:count], result[count : 2 * count]
            store(k1, 0, cosine[:, :LANES] + sine_part[:, LANES:])
            store(k1, 1, cosine[:, LANES:] - sine_part[:, :LANES])
            cosine, sine_part = result[2 * count : 3 * count], result[3 * count :]
            store(ROOT - k1, 0, cosine[:, :LANES] - sine_part[:, LANES:])
            store(ROOT - k1, 1, -cosine[:, LANES:] - sine_part[:, :LANES])
        else:
            section = section_ref[k1, : 2 * count, :]
            result = jnp.dot(section, split_data(real, 0, "hlh"), preferred_element_type=jnp.float32)
            store(k1, 0, result[:count])
            store(k1, 1, -result[count:])
    for k2 in range(count):
        for high in range(8):
            for part in range(2):
                at = (k2 * 8 + high) * 16 + part * 8
                out_ref[at : at + 8, :] = staged_ref[pl.ds((high * 16 + part) * 36 + k2, 8, stride=72), :]


def x_transform(first, second):
    outer, sections = x_tables()
    vmem, whole = pl.BlockSpec(memory_space=pltpu.VMEM), pl.BlockSpec(memory_space=pl.ANY)
    return pl.pallas_call(
        x_kernel,
        out_shape=jax.ShapeDtypeStruct((LENGTH, LANES), jnp.float32),
        in_specs=[vmem] * 3 + [whole] * 4,
        scratch_shapes=[
            pltpu.VMEM((ROOT * PITCH, LANES), jnp.float32),
            pltpu.VMEM((ROOT, PITCH, LANES), jnp.float32),
            pltpu.SemaphoreType.DMA((4,)),
        ],
        compiler_params=LIMIT,
        name="x_transform",
    )(jnp.asarray(outer), jnp.asarray(sections), first, *second)


def add(p, q):
    return (p[0] + q[0], p[1] + q[1])


def sub(p, q):
    return (p[0] - q[0], p[1] - q[1])


def turn_back(p):
    return (p[1], -p[0])


def times(p, angle):
    cosine, sine_part = math.cos(angle), math.sin(angle)
    return (p[0] * cosine - p[1] * sine_part, p[1] * cosine + p[0] * sine_part)


def four(p, q, r, s):
    even, odd = add(p, r), add(q, s)
    even_minus, odd_minus = sub(p, r), turn_back(sub(q, s))
    return add(even, odd), add(even_minus, odd_minus), sub(even, odd), sub(even_minus, odd_minus)


def sixteen(values):
    columns = []
    for n in range(4):
        column = four(*[values[4 * m + n] for m in range(4)])
        columns.append([times(v, -2.0 * math.pi * n * k / 16) if n * k else v for k, v in enumerate(column)])
    out = [None] * 16
    for k in range(4):
        for l, v in enumerate(four(*[columns[n][k] for n in range(4)])):
            out[k + 4 * l] = v
    return out


def y_kernel(symbol_x_ref, kz_ref, table_ref, cosine_ref, sine_ref, symbol_ref, lines_ref, out_ref, done_ref, staged_ref, sent):
    scale = -1.0 / math.sqrt(LENGTH * LENGTH)
    row = lax.broadcasted_iota(jnp.int32, (PLANES, 256), 0)
    kz = jnp.zeros((PLANES, 256), jnp.float32)
    for p in range(PLANES):
        kz = jnp.where(row == p, kz_ref[p], kz)
    for source in range(256):
        at = source // 4 % 2 * 128 + source // 8 * 4 + source % 4
        staged_ref[at * 24 : at * 24 + 16, :] = lines_ref[source * 16 : source * 16 + 16, :]
    device = 0
    for axis, size in zip(AXES, SIZES):
        device = device * size + lax.axis_index(axis)
    copies = []
    for j in range(8):
        rows = []
        for part in range(2):
            values = staged_ref[pl.ds(part * 8 + j, 256, stride=24), :]
            rows.append(values.T)
        lines = jnp.concatenate(rows, axis=0)
        even, odd = [
            jnp.dot(
                split_data(lines[:, i * LANES : (i + 1) * LANES], 1, "hlh"),
                table_ref[i],
                preferred_element_type=jnp.float32,
            )
            for i in range(2)
        ]
        values = []
        for n in range(16):
            halves = []
            for product in (even, odd):
                first = product[n * 8 : n * 8 + 8]
                second = product[LANES + n * 8 : LANES + n * 8 + 8]
                halves.append((first[:, :LANES] - second[:, LANES:], first[:, LANES:] + second[:, :LANES]))
            total, difference = add(*halves), sub(*halves)
            real, imag = [jnp.concatenate([total[i], difference[i]], axis=1) for i in range(2)]
            if n:
                cosine, sine_part = cosine_ref[n : n + 1, :], sine_ref[n : n + 1, :]
                real, imag = real * cosine - imag * sine_part, imag * cosine + real * sine_part
            values.append((real, imag))
        shift = kz + symbol_x_ref[device * 8 + j]
        for k, (real, imag) in enumerate(sixteen(values)):
            factor = scale / (shift + symbol_ref[k : k + 1, :])
            done_ref[j, 0, :, k * 256 : (k + 1) * 256] = real * factor
            done_ref[j, 1, :, k * 256 : (k + 1) * 256] = imag * factor
        copies.append(pltpu.make_async_copy(done_ref.at[j], out_ref.at[:, j], sent.at[j]))
        copies[-1].start()
    for copy in copies:
        copy.wait()


def y_transform(lines, kz_square):
    table, cosine, sine_part, symbol = y_tables()
    symbol_x = (4.0 * np.sin(np.pi * np.arange(KEPT) / LENGTH) ** 2).astype(np.float32)
    vmem = pl.BlockSpec(memory_space=pltpu.VMEM)
    smem = pl.BlockSpec(memory_space=pltpu.SMEM)
    return pl.pallas_call(
        y_kernel,
        out_shape=jax.ShapeDtypeStruct((2, 8, PLANES, LENGTH), jnp.float32),
        in_specs=[smem] * 2 + [vmem] * 5,
        out_specs=pl.BlockSpec(memory_space=pl.ANY),
        scratch_shapes=[
            pltpu.VMEM((8, 2, PLANES, LENGTH), jnp.float32),
            pltpu.VMEM((256 * 24, LANES), jnp.float32),
            pltpu.SemaphoreType.DMA((8,)),
        ],
        compiler_params=LIMIT,
        name="y_transform",
    )(
        jnp.asarray(symbol_x),
        kz_square,
        jnp.asarray(table),
        jnp.asarray(cosine),
        jnp.asarray(sine_part),
        jnp.asarray(symbol),
        lines,
    )


def around(parts):
    arrived = list(parts)
    for dz in (2, 1, 3):
        arrived[dz] = lax.ppermute(parts[dz], "zh", [(i, (i + dz) % 4) for i in range(4)])
    return arrived


def across(whole):
    inside = lax.axis_index("core") < SIZES[4]
    return lax.cond(inside, lambda v: lax.all_to_all(v, ("x", "y"), 0, 0, tiled=True), lambda v: v, whole)


def body(density, kz_square):
    *first, second = pack(density)
    first = around(first)
    second = split(across(second))
    first = across(join(first, second[0]))
    second = around(second)
    spectrum = x_transform(first, second)
    lines = lax.all_to_all(spectrum.reshape(256, 16, LANES), AXES, 0, 0, tiled=True)
    return y_transform(lines.reshape(LENGTH, LANES), kz_square)


def solution(mesh):
    fine = Mesh(mesh.devices.reshape(SIZES), AXES)
    in_specs = (P(AXES[:3], AXES[3:]), P())
    out_specs = P(None, AXES, None, None)
    return jax.shard_map(body, mesh=fine, in_specs=in_specs, out_specs=out_specs, check_vma=False)
```

```python
import functools
import math

import jax
import jax.numpy as jnp
import ml_dtypes
import numpy as np
from jax import lax
from jax.experimental import pallas as pl
from jax.experimental.pallas import tpu as pltpu
from jax.sharding import Mesh
from jax.sharding import PartitionSpec as P

LENGTH = 4096
KEPT = 2048
ROOT = 64
LANES = 128
PITCH = 72
ROWS = 32
PLANES = 8
AXES = ("zh", "x", "y", "zl", "core")
SIZES = (4, 4, 4, 2, 2)
LIMIT = pltpu.CompilerParams(vmem_limit_bytes=24 << 20)


def split_table(table, axis, order):
    high = table.astype(ml_dtypes.bfloat16)
    low = (table - high.astype(np.float64)).astype(ml_dtypes.bfloat16)
    parts = {"h": high, "l": low}
    return np.concatenate([parts[name] for name in order], axis=axis)


def split_data(values, axis, order):
    high = values.astype(jnp.bfloat16)
    low = (values - high.astype(jnp.float32)).astype(jnp.bfloat16)
    parts = {"h": high, "l": low}
    return jnp.concatenate([parts[name] for name in order], axis=axis)


@functools.cache
def x_tables():
    a = np.arange(ROOT)
    first = 2.0 * np.pi * np.outer(np.arange(ROOT // 2 + 1), a) / ROOT
    outer = np.concatenate([np.cos(first), -np.sin(first[1 : ROOT // 2])], axis=0)
    sections = []
    k2 = np.arange(KEPT // ROOT)
    for k1 in range(ROOT // 2 + 1):
        rows = []
        for k in (k1, (ROOT - k1) % ROOT):
            angle = 2.0 * np.pi * np.outer(k + ROOT * k2, a) / LENGTH
            rows += [np.cos(angle), np.sin(angle)]
        sections.append(np.concatenate(rows, axis=0))
    return split_table(outer, 1, "hhl"), split_table(np.stack(sections), 2, "hhl")


@functools.cache
def y_tables():
    source = np.arange(256)
    place = (source % 4) * 64 + source // 4
    tables = []
    for odd in range(2):
        angle = 2.0 * np.pi * np.outer(place[place % 2 == odd], np.arange(LANES)) / 256
        tables.append(split_table(np.concatenate([np.cos(angle), -np.sin(angle)], axis=1), 0, "hhl"))
    turn = 2.0 * np.pi * np.outer(np.arange(16), np.arange(256)) / LENGTH
    wave = np.arange(LENGTH).reshape(16, 256)
    symbol = 4.0 * np.sin(np.pi * wave / LENGTH) ** 2
    return (
        np.stack(tables),
        np.cos(turn).astype(np.float32),
        (-np.sin(turn)).astype(np.float32),
        symbol.astype(np.float32),
    )


def pack_kernel(density_ref, *out_refs):
    zh = lax.axis_index("zh")
    for dz in range(4):
        base = ((zh + dz) & 3) * (16 * LANES)
        for xy in range(16):
            columns = pl.ds(pl.multiple_of(base + xy * LANES, LANES), LANES)
            out_refs[dz][xy] = density_ref[:ROWS, columns]
            out_refs[4][xy, dz] = density_ref[ROWS:, columns]


def join_kernel(earlier_ref, *refs):
    for slot, ref in enumerate(refs[:-1]):
        refs[-1][:, slot] = ref[...]


def split_kernel(in_ref, *out_refs):
    for slot, ref in enumerate(out_refs):
        ref[...] = in_ref[:, slot]


def floats(*shape):
    return pltpu.VMEM(shape, jnp.float32)


def pack(density):
    out_shape = [floats(16, ROWS, LANES)] * 4 + [floats(16, 4, ROWS, LANES)]
    return pl.pallas_call(pack_kernel, out_shape=out_shape, name="pack", compiler_params=LIMIT)(density)


def join(parts, earlier):
    in_specs = [pl.BlockSpec(memory_space=pl.ANY)] + [pl.BlockSpec(memory_space=pltpu.VMEM)] * 4
    return pl.pallas_call(
        join_kernel, out_shape=floats(16, 4, ROWS, LANES), in_specs=in_specs, name="join", compiler_params=LIMIT
    )(earlier, *parts)


def split(whole):
    return pl.pallas_call(
        split_kernel, out_shape=[floats(16, ROWS, LANES)] * 4, name="split", compiler_params=LIMIT
    )(whole)


def x_kernel(outer_ref, section_ref, first_ref, *refs):
    second_refs, (out_ref, mixed_ref, places_ref, arrived) = refs[:4], refs[4:]
    staged_ref = places_ref.reshape(ROOT * PITCH, LANES)
    outer = outer_ref[...]
    zh = lax.axis_index("zh")
    copies = []
    for dz in range(4):
        place = places_ref.at[pl.ds(((zh - dz) & 3) * 16, 16), pl.ds(ROWS, ROWS), :]
        copies.append(pltpu.make_async_copy(second_refs[dz], place, arrived.at[dz]))
        copies[-1].start()
    for dz in range(4):
        for xy in range(16):
            places_ref[((zh - dz) & 3) * 16 + xy, :ROWS, :] = first_ref[xy, dz]
    for b in range(0, ROOT, 2):
        if b == ROWS:
            for copy in copies:
                copy.wait()
        pair = jnp.concatenate(
            [staged_ref[pl.ds(b + i, ROOT, stride=PITCH), :] for i in range(2)], axis=1
        )
        mixed = jnp.dot(outer, split_data(pair, 0, "hlh"), preferred_element_type=jnp.float32)
        for i in range(2):
            mixed_ref[pl.ds(b + i, ROOT, stride=PITCH), :] = mixed[:, i * LANES : (i + 1) * LANES]
    count = KEPT // ROOT

    def store(k1, part, values):
        staged_ref[(k1 * 2 + part) * 36 : (k1 * 2 + part) * 36 + count, :] = values

    for k1 in range(ROOT // 2 + 1):
        real = mixed_ref[k1 * PITCH : k1 * PITCH + ROOT, :]
        if 0 < k1 < ROOT // 2:
            at = (ROOT // 2 + k1) * PITCH
            values = jnp.concatenate([real, mixed_ref[at : at + ROOT, :]], axis=1)
            result = jnp.dot(section_ref[k1], split_data(values, 0, "hlh"), preferred_element_type=jnp.float32)
            cosine, sine_part = result[:count], result[count : 2 * count]
            store(k1, 0, cosine[:, :LANES] + sine_part[:, LANES:])
            store(k1, 1, cosine[:, LANES:] - sine_part[:, :LANES])
            cosine, sine_part = result[2 * count : 3 * count], result[3 * count :]
            store(ROOT - k1, 0, cosine[:, :LANES] - sine_part[:, LANES:])
            store(ROOT - k1, 1, -cosine[:, LANES:] - sine_part[:, :LANES])
        else:
            section = section_ref[k1, : 2 * count, :]
            result = jnp.dot(section, split_data(real, 0, "hlh"), preferred_element_type=jnp.float32)
            store(k1, 0, result[:count])
            store(k1, 1, -result[count:])
    for k2 in range(count):
        for high in range(8):
            for part in range(2):
                at = (k2 * 8 + high) * 16 + part * 8
                out_ref[at : at + 8, :] = staged_ref[pl.ds((high * 16 + part) * 36 + k2, 8, stride=72), :]


def x_transform(first, second):
    outer, sections = x_tables()
    vmem, whole = pl.BlockSpec(memory_space=pltpu.VMEM), pl.BlockSpec(memory_space=pl.ANY)
    return pl.pallas_call(
        x_kernel,
        out_shape=jax.ShapeDtypeStruct((LENGTH, LANES), jnp.float32),
        in_specs=[vmem] * 3 + [whole] * 4,
        scratch_shapes=[
            pltpu.VMEM((ROOT * PITCH, LANES), jnp.float32),
            pltpu.VMEM((ROOT, PITCH, LANES), jnp.float32),
            pltpu.SemaphoreType.DMA((4,)),
        ],
        compiler_params=LIMIT,
        name="x_transform",
    )(jnp.asarray(outer), jnp.asarray(sections), first, *second)


def add(p, q):
    return (p[0] + q[0], p[1] + q[1])


def sub(p, q):
    return (p[0] - q[0], p[1] - q[1])


def turn_back(p):
    return (p[1], -p[0])


def times(p, angle):
    cosine, sine_part = math.cos(angle), math.sin(angle)
    return (p[0] * cosine - p[1] * sine_part, p[1] * cosine + p[0] * sine_part)


def four(p, q, r, s):
    even, odd = add(p, r), add(q, s)
    even_minus, odd_minus = sub(p, r), turn_back(sub(q, s))
    return add(even, odd), add(even_minus, odd_minus), sub(even, odd), sub(even_minus, odd_minus)


def sixteen(values):
    columns = []
    for n in range(4):
        column = four(*[values[4 * m + n] for m in range(4)])
        columns.append([times(v, -2.0 * math.pi * n * k / 16) if n * k else v for k, v in enumerate(column)])
    out = [None] * 16
    for k in range(4):
        for l, v in enumerate(four(*[columns[n][k] for n in range(4)])):
            out[k + 4 * l] = v
    return out


def y_kernel(symbol_x_ref, kz_ref, table_ref, cosine_ref, sine_ref, symbol_ref, lines_ref, out_ref, done_ref, staged_ref, sent):
    scale = -1.0 / math.sqrt(LENGTH * LENGTH)
    row = lax.broadcasted_iota(jnp.int32, (PLANES, 256), 0)
    kz = jnp.zeros((PLANES, 256), jnp.float32)
    for p in range(PLANES):
        kz = jnp.where(row == p, kz_ref[p], kz)
    for source in range(256):
        at = source // 4 % 2 * 128 + source // 8 * 4 + source % 4
        staged_ref[at * 24 : at * 24 + 16, :] = lines_ref[source * 16 : source * 16 + 16, :]
    device = 0
    for axis, size in zip(AXES, SIZES):
        device = device * size + lax.axis_index(axis)
    symbol_x = symbol_x_ref[pl.ds(device, 1), :]
    copies = []
    for j in range(8):
        rows = []
        for part in range(2):
            values = staged_ref[pl.ds(part * 8 + j, 256, stride=24), :]
            rows.append(values.T)
        lines = jnp.concatenate(rows, axis=0)
        even, odd = [
            jnp.dot(
                split_data(lines[:, i * LANES : (i + 1) * LANES], 1, "hlh"),
                table_ref[i],
                preferred_element_type=jnp.float32,
            )
            for i in range(2)
        ]
        values = []
        for n in range(16):
            halves = []
            for product in (even, odd):
                first = product[n * 8 : n * 8 + 8]
                second = product[LANES + n * 8 : LANES + n * 8 + 8]
                halves.append((first[:, :LANES] - second[:, LANES:], first[:, LANES:] + second[:, :LANES]))
            total, difference = add(*halves), sub(*halves)
            real, imag = [jnp.concatenate([total[i], difference[i]], axis=1) for i in range(2)]
            if n:
                cosine, sine_part = cosine_ref[n : n + 1, :], sine_ref[n : n + 1, :]
                real, imag = real * cosine - imag * sine_part, imag * cosine + real * sine_part
            values.append((real, imag))
        shift = kz + symbol_x[:, j : j + 1]
        for k, (real, imag) in enumerate(sixteen(values)):
            factor = scale / (shift + symbol_ref[k : k + 1, :])
            done_ref[j, 0, :, k * 256 : (k + 1) * 256] = real * factor
            done_ref[j, 1, :, k * 256 : (k + 1) * 256] = imag * factor
            if k == 15 or (j, k) == (7, 7):
                part = pl.ds(2048 * (k // 15), 2048) if j == 7 else pl.ds(0, LENGTH)
                source, target = done_ref.at[j, :, :, part], out_ref.at[:, j, :, part]
                copies.append(pltpu.make_async_copy(source, target, sent.at[len(copies)]))
                copies[-1].start()
    for copy in copies:
        copy.wait()


def y_transform(lines, kz_square):
    table, cosine, sine_part, symbol = y_tables()
    symbol_x = (4.0 * np.sin(np.pi * np.arange(KEPT) / LENGTH) ** 2).astype(np.float32)
    symbol_x = np.pad(symbol_x.reshape(256, 8), ((0, 0), (0, LANES - 8)))
    vmem = pl.BlockSpec(memory_space=pltpu.VMEM)
    smem = pl.BlockSpec(memory_space=pltpu.SMEM)
    return pl.pallas_call(
        y_kernel,
        out_shape=jax.ShapeDtypeStruct((2, 8, PLANES, LENGTH), jnp.float32),
        in_specs=[vmem, smem] + [vmem] * 5,
        out_specs=pl.BlockSpec(memory_space=pl.ANY),
        scratch_shapes=[
            pltpu.VMEM((8, 2, PLANES, LENGTH), jnp.float32),
            pltpu.VMEM((256 * 24, LANES), jnp.float32),
            pltpu.SemaphoreType.DMA((9,)),
        ],
        compiler_params=LIMIT,
        name="y_transform",
    )(
        jnp.asarray(symbol_x),
        kz_square,
        jnp.asarray(table),
        jnp.asarray(cosine),
        jnp.asarray(sine_part),
        jnp.asarray(symbol),
        lines,
    )


def around(parts):
    arrived = list(parts)
    for dz in (2, 1, 3):
        arrived[dz] = lax.ppermute(parts[dz], "zh", [(i, (i + dz) % 4) for i in range(4)])
    return arrived


def across(whole):
    inside = lax.axis_index("core") < SIZES[4]
    return lax.cond(inside, lambda v: lax.all_to_all(v, ("x", "y"), 0, 0, tiled=True), lambda v: v, whole)


def body(density, kz_square):
    *first, second = pack(density)
    first = around(first)
    second = split(across(second))
    first = across(join(first, second[0]))
    second = around(second)
    spectrum = x_transform(first, second)
    lines = lax.all_to_all(spectrum.reshape(256, 16, LANES), AXES, 0, 0, tiled=True)
    return y_transform(lines.reshape(LENGTH, LANES), kz_square)


def solution(mesh):
    fine = Mesh(mesh.devices.reshape(SIZES), AXES)
    in_specs = (P(AXES[:3], AXES[3:]), P())
    out_specs = P(None, AXES, None, None)
    return jax.shard_map(body, mesh=fine, in_specs=in_specs, out_specs=out_specs, check_vma=False)
```
